128 devices in a mesh: dp: 32 (over y, z, core), tensor: 4 (over x).
Axes of the slice: x: 4, y: 4, z: 4, core: 2. Of those that a mesh axis runs over, the one named last changes fastest.
Arguments:
- queries: bfloat16 [4096, 4096], P('dp', 'tensor'), may hold values from -5 to 5
- rotated_key_rows: bfloat16 [4096, 512], P('dp', 'tensor'), may hold values from -5 to 5
- value_matrix: bfloat16 [4096, 512], P('dp', 'tensor'), may hold values from -4 to 4
- residual: bfloat16 [4096, 4096], P('dp', 'tensor'), may hold values from -10.5 to 10.5
- lengths: int32 [64, 4], replicated, may hold values from 1 to 32, 64 in all within a row
- move_plan: int32 [64], replicated, may hold values from 0 to 31, as said below
- out_weight: bfloat16 [4096, 4096], P('tensor', 'dp'), may hold values from -0.09375 to 0.09375
- norm_gain: float32 [4096], P('tensor'), may hold values from 0.1 to 1.9
- routes: int32 [4096, 8], P('dp'), may hold values from 0 to 63, as said below
- bin_slots: int32 [4096, 8], P('dp'), may hold values from 0 to 15, as said below
- dropped: int32 [4096, 8], P('dp'), may hold values from 0 to 1, as said below
- route_weight: float32 [4096, 8], P('dp'), may hold values from 0.05 to 0.4
- gate_weight: bfloat16 [64, 4096, 1536], P('dp', None, 'tensor'), may hold values from -0.09375 to 0.09375
- up_weight: bfloat16 [64, 4096, 1536], P('dp', None, 'tensor'), may hold values from -0.09375 to 0.09375
- down_weight: bfloat16 [64, 1536, 4096], P('dp', 'tensor'), may hold values from -0.15625 to 0.15625
Outputs:
- stream: bfloat16 [4096, 4096], P('dp', 'tensor')
- expert_mix: bfloat16 [4096, 4096], P('dp', 'tensor')
The draws below stay inside these ranges and needn't reach their ends.
Inputs may be any that keep to these rules, and one draw needn't show every extreme that they name: `lengths`: each row sums to 64; the largest entry of every row is exactly 32. Pack p goes to index move_plan[p] of dp. For each s, the packs with p % 2 = s go to different indices, and the 2 packs of one index go to different indices. `routes`: each row names 8 different experts. `bin_slots`: among the entries of the rows of one index of dp that are kept for one expert, the slots are different. 1 marks a dropped entry. The rows of one index of dp keep at most 16 entries for any expert; in every draw one expert keeps exactly 16 entries from every index, and on every index some expert is named by more than 16 entries.
All inputs are finite; a program needn't handle non-finite values.
Results may differ from the reference program's by a relative error of at most 0.03.
Values may be sent and summed in bfloat16 or wider, within the bound.
No kernel may reach another device: no remote copies, remote signals or barrier semaphores. Data moves between devices by JAX's collectives and lax.ppermute only.
A program may use at most 128 MiB of HBM per device.

```python
import math
import jax
import jax.numpy as jnp
import numpy as np
from jax import lax

D = 4096
HQ = 32
KEY_HEADS = 4
HEAD_WIDTH = 128
FF = 1536
TOP = 8
SEQ_DEV = 2
PACK_ROWS = 64
DOCS = 4
QUERY_PER_KEY = 8
MOST = 32
TOK_DEV = 128
TOKEN_COUNT = 4096
PACK_COUNT = 64
EXPERTS = 64
CAP = 16
FF_PART = 384
N_DP = 32


def route_tables(key):
    popular_key, favored_key, score_key, order_key = jax.random.split(key, 4)
    device_count = TOKEN_COUNT // TOK_DEV
    popular = jax.random.randint(popular_key, (EXPERTS,), 1, 5)
    favored = jax.random.randint(favored_key, (), 0, EXPERTS)
    baseline = jax.random.randint(score_key, (TOKEN_COUNT, EXPERTS), 0, 4096)
    labels = jnp.arange(EXPERTS, dtype=jnp.int32)
    scores = baseline * popular[None, :] * EXPERTS + labels[None, :]
    priority = jax.random.randint(order_key, (device_count, TOK_DEV), 0, 1 << 20)
    ordering = jnp.argsort(priority, axis=1, stable=True)
    position = jnp.argsort(ordering, axis=1, stable=True)
    favored_rows = (position < CAP + CAP // 2 + 1).reshape(TOKEN_COUNT)
    scores = scores + jnp.where(favored_rows[:, None] & (labels[None, :] == favored), 1 << 24, 0)
    routes = lax.top_k(scores, TOP)[1].astype(jnp.int32)
    flattened = routes.reshape(device_count, TOK_DEV * TOP)
    matches = (flattened[:, :, None] == labels[None, None, :]).astype(jnp.int32)
    earlier = jnp.cumsum(matches, axis=1) - matches
    arrival = jnp.sum(earlier * matches, axis=2).reshape(TOKEN_COUNT, TOP)
    dropped = (arrival >= CAP).astype(jnp.int32)
    slots = jnp.where(arrival < CAP, arrival, arrival % CAP).astype(jnp.int32)
    return (routes, slots, dropped)


def draw_queries(key, part):
    key = jax.random.fold_in(key, 11)
    sampled_draw = jnp.clip(jax.random.normal(key, (TOKEN_COUNT, KEY_HEADS, QUERY_PER_KEY, HEAD_WIDTH)), -4.0, 4.0)
    return sampled_draw.reshape(TOKEN_COUNT, HQ * HEAD_WIDTH).astype(jnp.bfloat16)


def draw_rotated_key_rows(key, part):
    key = jax.random.fold_in(key, 12)
    sampled_draw = jnp.clip(jax.random.normal(key, (TOKEN_COUNT, KEY_HEADS, HEAD_WIDTH)), -4.0, 4.0)
    return sampled_draw.reshape(TOKEN_COUNT, KEY_HEADS * HEAD_WIDTH).astype(jnp.bfloat16)


def draw_residual(key, part):
    key = jax.random.fold_in(key, 21)
    row_key = jax.random.fold_in(key, 0)
    rough_key = jax.random.fold_in(key, 2)
    row_scale = jnp.exp(jax.random.uniform(row_key, (TOKEN_COUNT, 1), minval=jnp.log(0.25), maxval=jnp.log(2.5)))
    col_scale = 0.55 * jnp.exp(jnp.log(3.0) * jnp.arange(D, dtype=jnp.float32) / D)
    sampled_draw = jnp.clip(jax.random.normal(rough_key, (TOKEN_COUNT, D)), -2.5, 2.5)
    return (sampled_draw * row_scale * col_scale[None, :]).astype(jnp.bfloat16)


def draw_move_plan(key, part):
    key = jax.random.fold_in(key, 31)
    outer_key, inner_key = jax.random.split(key, 2)
    device_count = TOKEN_COUNT // TOK_DEV
    outer_perm = jax.random.permutation(outer_key, device_count)
    inner_perm = jax.random.permutation(inner_key, device_count)
    slot_index = jnp.arange(SEQ_DEV, dtype=jnp.int32)
    destination = outer_perm[(inner_perm[:, None] + slot_index[None, :]) % device_count]
    return destination.reshape(PACK_COUNT).astype(jnp.int32)


def draw_routes(key, part):
    tables = route_tables(key)
    return tables[0]


def draw_bin_slots(key, part):
    tables = route_tables(key)
    return tables[1]


def draw_dropped(key, part):
    tables = route_tables(key)
    return tables[2]


def block_levels(key, extent, cuts, low, largest):
    gain, own = 1.0, jax.random.fold_in(key, 6)
    for axis_at, shards_of in cuts:
        heights = jnp.exp(jax.random.uniform(jax.random.fold_in(own, axis_at), (shards_of,), jnp.float32, low / len(cuts), largest / len(cuts)))
        gain = gain * jnp.repeat(heights, extent[axis_at] // shards_of).reshape([-1 if axis == axis_at else 1 for axis in range(len(extent))])
    return gain


def split_up(count, total, limit, slope):
    loads = [(1 << 20) // math.isqrt(rank ** slope) + 1 for rank in range(2, count + 1)]
    surplus, holding = total - limit - (count - 1), [1] * (count - 1)
    while surplus > 0:
        movable = [i for i in range(count - 1) if holding[i] < limit]
        mass, remaining = sum([loads[i] for i in movable]), surplus
        for i in movable:
            more = min(limit - holding[i], max(1, remaining * loads[i] // mass), surplus)
            holding[i] = holding[i] + more
            surplus = surplus - more
    return np.array([limit] + holding)


def uneven(key, amount, total, limit, slope):
    if amount == 2:
        one = jax.random.randint(key, (), max(1, total - limit), min(limit, total - 1) + 1)
        return jnp.stack([one, total - one])
    sizes = jnp.asarray(split_up(amount, total, limit, slope), jnp.int32)
    twos = (amount - 1) // 2
    donor, taker = sizes[1:1 + 2 * twos:2], sizes[2:2 + 2 * twos:2]
    margin = jnp.minimum(donor - 1, limit - taker)
    moved = jax.random.randint(jax.random.fold_in(key, 1), (twos,), 0, 1 << 20) % (margin + 1)
    sizes = sizes.at[1:1 + 2 * twos:2].set(donor - moved).at[2:2 + 2 * twos:2].set(taker + moved)
    return sizes[jax.random.permutation(jax.random.fold_in(key, 2), amount)]


def normal_values(stream_key, extent, width, most, cuts=(), kind=jnp.bfloat16):
    loudness = block_levels(stream_key, extent, cuts, -0.22, 0.18) if cuts else 1.0
    result = jax.random.normal(stream_key, extent, jnp.float32) * width * loudness
    return jnp.minimum(jnp.maximum(result, -most), most).astype(kind)


def setup_inputs(seed: int = 0) -> dict:
    streams_of = jax.random.split(jax.random.key(seed), 16)
    queries = draw_queries(jax.random.fold_in(streams_of[15], 71), 0)
    rotated_key_rows = draw_rotated_key_rows(jax.random.fold_in(streams_of[15], 71), 0)
    value_matrix = normal_values(streams_of[2], (TOKEN_COUNT, KEY_HEADS * HEAD_WIDTH), 1.0, 4.0, ((0, 32), (1, 4)))
    residual = draw_residual(jax.random.fold_in(streams_of[15], 71), 0)
    lengths = jax.vmap(lambda own: uneven(own, DOCS, PACK_ROWS, MOST, 2))(jax.random.split(streams_of[4], PACK_COUNT)).reshape((PACK_COUNT, DOCS)).astype(jnp.int32)
    move_plan = draw_move_plan(jax.random.fold_in(streams_of[15], 71), 0)
    out_weight = normal_values(streams_of[6], (HQ * HEAD_WIDTH, D), (HQ * HEAD_WIDTH) ** -0.5, 0.09375, ((0, 4), (1, 32)))
    norm_gain = jnp.clip(1.0 + 0.18 * jax.random.normal(streams_of[7], (D,), jnp.float32), 0.1, 1.9)
    routes = draw_routes(jax.random.fold_in(streams_of[15], 71), 0)
    bin_slots = draw_bin_slots(jax.random.fold_in(streams_of[15], 71), 0)
    dropped = draw_dropped(jax.random.fold_in(streams_of[15], 71), 0)
    route_weight = jnp.clip(0.05 + 0.35 * jax.random.uniform(streams_of[11], (TOKEN_COUNT, TOP), jnp.float32) ** block_levels(streams_of[11], (TOKEN_COUNT, TOP), ((0, 32),), -0.2, 0.2), 0.05, 0.4)
    gate_weight = normal_values(streams_of[12], (EXPERTS, D, FF), D ** -0.5, 0.09375, ((0, 32), (2, 4)))
    up_weight = normal_values(streams_of[13], (EXPERTS, D, FF), D ** -0.5, 0.09375, ((0, 32), (2, 4)))
    down_weight = normal_values(streams_of[14], (EXPERTS, FF, D), FF ** -0.5, 0.15625, ((0, 32), (1, 4)))
    return {"queries": queries, "rotated_key_rows": rotated_key_rows, "value_matrix": value_matrix, "residual": residual, "lengths": lengths, "move_plan": move_plan, "out_weight": out_weight, "norm_gain": norm_gain, "routes": routes, "bin_slots": bin_slots, "dropped": dropped, "route_weight": route_weight, "gate_weight": gate_weight, "up_weight": up_weight, "down_weight": down_weight}


def document_labels(lengths):
    doc_ends = jnp.cumsum(lengths, axis=1)
    position = jnp.arange(PACK_ROWS, dtype=jnp.int32)
    return lax.optimization_barrier(jnp.sum((position[None, :, None] >= doc_ends[:, None, :]).astype(jnp.int32), axis=2))

def expert_layer(operands):
    inputs, gate_part, up_part, down_part = operands
    gated = jnp.dot(inputs, gate_part, preferred_element_type=jnp.float32)
    upward = jnp.dot(inputs, up_part, preferred_element_type=jnp.float32)
    hidden = (jax.nn.silu(gated) * upward).astype(jnp.bfloat16)
    total = jnp.zeros((inputs.shape[0], D), jnp.float32)
    for block_index in range(FF // FF_PART):
        lower = block_index * FF_PART
        partial_value = jnp.dot(hidden[:, lower:lower + FF_PART], down_part[lower:lower + FF_PART], preferred_element_type=jnp.float32).astype(jnp.bfloat16)
        total = total + lax.optimization_barrier(partial_value).astype(jnp.float32)
    return total.astype(jnp.bfloat16)

def reference(queries, rotated_key_rows, value_matrix, residual, lengths, move_plan, out_weight, norm_gain, routes, bin_slots, dropped, route_weight, gate_weight, up_weight, down_weight):
    doc_label = document_labels(lengths)
    position = jnp.arange(PACK_ROWS, dtype=jnp.int32)
    visible = (doc_label[:, :, None] == doc_label[:, None, :]) & (position[:, None] >= position[None, :])[None]
    query_head_count = queries.astype(jnp.float32).reshape(PACK_COUNT, PACK_ROWS, KEY_HEADS, QUERY_PER_KEY, HEAD_WIDTH)
    key_head_count = rotated_key_rows.astype(jnp.float32).reshape(PACK_COUNT, PACK_ROWS, KEY_HEADS, HEAD_WIDTH)
    value_head_count = value_matrix.astype(jnp.float32).reshape(PACK_COUNT, PACK_ROWS, KEY_HEADS, HEAD_WIDTH)
    scores = jnp.einsum('pingd,pjnd->pngij', query_head_count, key_head_count) * HEAD_WIDTH ** (-0.5)
    masked = jnp.where(visible[:, None, None], scores, -1e+30)
    row_max = lax.optimization_barrier(jnp.max(masked, axis=-1, keepdims=True))
    exp_scores = jnp.exp(masked - row_max)
    soft_weights = (exp_scores / lax.optimization_barrier(jnp.sum(exp_scores, axis=-1, keepdims=True))).astype(jnp.bfloat16)
    attended = jnp.einsum('pngij,pjnd->pingd', soft_weights.astype(jnp.float32), value_head_count)
    attended = attended.reshape(TOKEN_COUNT, HQ * HEAD_WIDTH).astype(jnp.bfloat16)
    merged = (residual.astype(jnp.float32) + jnp.dot(attended, out_weight, preferred_element_type=jnp.float32)).astype(jnp.bfloat16)
    pack_index = jnp.arange(PACK_COUNT, dtype=jnp.int32)
    destination = move_plan * SEQ_DEV + pack_index % SEQ_DEV
    stream = jnp.zeros((PACK_COUNT, PACK_ROWS, D), jnp.bfloat16).at[destination].set(merged.reshape(PACK_COUNT, PACK_ROWS, D)).reshape(TOKEN_COUNT, D)
    widened = stream.astype(jnp.float32)
    normed = (widened * lax.rsqrt(lax.optimization_barrier(jnp.mean(widened * widened, axis=1, keepdims=True)) + 1e-06) * norm_gain[None, :]).astype(jnp.bfloat16)
    device = jnp.arange(TOKEN_COUNT, dtype=jnp.int32) // TOK_DEV
    kept_mask = (1 - dropped).astype(jnp.float32)
    segment = (routes * N_DP + device[:, None]) * CAP + bin_slots
    normed_wide = normed.astype(jnp.float32)
    bin_rows = jnp.zeros((EXPERTS * N_DP * CAP, D), jnp.float32)
    for route_index in range(TOP):
        bin_rows = bin_rows + jax.ops.segment_sum(normed_wide * kept_mask[:, route_index, None], segment[:, route_index], num_segments=EXPERTS * N_DP * CAP)
    bin_rows = bin_rows.astype(jnp.bfloat16).reshape(EXPERTS, N_DP * CAP, D)
    returned = lax.map(expert_layer, (bin_rows, gate_weight, up_weight, down_weight)).reshape(EXPERTS * N_DP * CAP, D)
    expert_mix = jnp.zeros((TOKEN_COUNT, D), jnp.float32)
    for route_index in range(TOP):
        coefficient = kept_mask[:, route_index] * route_weight[:, route_index]
        expert_mix = expert_mix + coefficient[:, None] * jnp.take(returned, segment[:, route_index], axis=0).astype(jnp.float32)
    return (stream, expert_mix.astype(jnp.bfloat16))
```

```python
import jax
import jax.numpy as jnp
from jax import lax
from jax.sharding import Mesh, PartitionSpec as P

D = 4096
HEAD_WIDTH = 128
PACK_ROWS = 64
QUERY_PER_KEY = 8
DP = ("y", "z", "core")
ROWS = 128
CAP = 16
F32 = jnp.float32
BF16 = jnp.bfloat16

RIGHT = [(i, (i + 1) % 4) for i in range(4)]
LEFT = [(i, (i - 1) % 4) for i in range(4)]


def iota(shape, dim):
    return lax.broadcasted_iota(jnp.int32, shape, dim)


def pick(one_hot, rows):
    return jnp.dot(one_hot, rows, preferred_element_type=F32).astype(rows.dtype)


def attend(queries, keys, values, ends):
    position = iota((ROWS, 1), 0)
    pack = position // PACK_ROWS
    inner = position % PACK_ROWS
    row_ends = jnp.where(pack == 0, ends[0][None, :], ends[1][None, :])
    label = pack * 8 + jnp.sum((inner >= row_ends).astype(jnp.int32), axis=1, keepdims=True)
    visible = (label == label.reshape(1, ROWS)) & (position >= position.reshape(1, ROWS))
    heads = queries.reshape(ROWS, QUERY_PER_KEY, HEAD_WIDTH)
    scores = jnp.einsum("igd,jd->gij", heads, keys, preferred_element_type=F32) * HEAD_WIDTH**-0.5
    masked = jnp.where(visible[None], scores, -1e30)
    top = jnp.max(masked, axis=-1, keepdims=True)
    exps = jnp.exp(masked - top)
    probs = (exps / jnp.sum(exps, axis=-1, keepdims=True)).astype(BF16)
    out = jnp.einsum("gij,jd->igd", probs, values, preferred_element_type=F32)
    return out.reshape(ROWS, QUERY_PER_KEY * HEAD_WIDTH).astype(BF16)


def ring_gather(block, axis):
    half = block.shape[0] // 2
    from_left = lax.ppermute(block, axis, RIGHT)
    from_right = lax.ppermute(block, axis, LEFT)
    far_top = lax.ppermute(from_left[:half], axis, RIGHT)
    far_low = lax.ppermute(from_right[half:], axis, LEFT)
    return block, from_right, jnp.concatenate([far_top, far_low], axis=0), from_left


def ring_scatter(far, to_right, to_left, axis):
    half = far.shape[0] // 2
    top = lax.ppermute(far[:half], axis, RIGHT)
    low = lax.ppermute(far[half:], axis, LEFT)
    right_low = lax.ppermute(to_right[half:].astype(BF16), axis, RIGHT)
    left_top = lax.ppermute(to_left[:half].astype(BF16), axis, LEFT)
    right_top = lax.ppermute((to_right[:half] + top.astype(F32)).astype(BF16), axis, RIGHT)
    left_low = lax.ppermute((to_left[half:] + low.astype(F32)).astype(BF16), axis, LEFT)
    return (
        jnp.concatenate([right_top, right_low], axis=0),
        jnp.concatenate([left_top, left_low], axis=0),
    )


def per_device(
    queries,
    rotated_key_rows,
    value_matrix,
    residual,
    lengths,
    move_plan,
    out_weight,
    norm_gain,
    routes,
    bin_slots,
    dropped,
    route_weight,
    gate_weight,
    up_weight,
    down_weight,
):
    x = lax.axis_index("tensor")
    d = lax.axis_index(DP)

    weight = lax.all_gather(out_weight, ("y", "core"), axis=1, tiled=True)
    gains = lax.all_gather(norm_gain, "tensor", axis=0, tiled=False)

    own = lax.dynamic_slice_in_dim(lengths, 2 * d, 2, axis=0)
    e0 = own[:, 0:1]
    e1 = e0 + own[:, 1:2]
    e2 = e1 + own[:, 2:3]
    e3 = e2 + own[:, 3:4]
    attended = attend(
        queries, rotated_key_rows, value_matrix, jnp.concatenate([e0, e1, e2, e3], axis=1)
    )

    z = lax.axis_index("z")
    gathered = ring_gather(attended, "z")
    stacked = jnp.stack(gathered, axis=0)
    everyone = jnp.concatenate([stacked, stacked], axis=0)
    tokens = lax.dynamic_slice_in_dim(everyone, (4 - z) % 4, 4, axis=0).reshape(4 * ROWS, 1024)

    def project(distance):
        columns = lax.dynamic_slice_in_dim(weight, ((x + distance) % 4) * 256, 256, axis=1)
        return jnp.dot(tokens, columns, preferred_element_type=F32)

    res = lax.all_to_all(residual.reshape(ROWS, 4, 256).swapaxes(0, 1), "z", 0, 0, tiled=True)
    res = res.reshape(4 * ROWS, 256)
    one, two = ring_scatter(project(2).astype(BF16), project(1), project(3), "tensor")
    merged = (res.astype(F32) + (project(0) + one.astype(F32) + two.astype(F32))).astype(BF16)

    to = iota((512, 512), 0)
    at = iota((512, 512), 1)
    spread = (
        ((at // 2) % 32 == to // 16) & (at // 64 == (to // 2) % 8) & (at % 2 == to % 2)
    ).astype(BF16)
    sent = pick(spread, merged).reshape(32, 16, 256)
    middle = lax.all_to_all(sent, DP, 0, 0, tiled=True).reshape(512, 256)
    plan = move_plan.reshape(32, 2)
    source = jnp.sum(
        jnp.where(plan[None] == iota((32, 32, 2), 0), iota((32, 32, 2), 1), 0), axis=1
    )
    pack_source = jnp.broadcast_to(source[:, None, :, None], (32, 4, 2, 2)).reshape(512, 1)
    at_source = (at // 128) * 8 + ((at // 4) % 4) * 2 + (at // 16) % 2
    onward = (
        (pack_source == at_source)
        & ((to // 4) % 4 == (at // 32) % 4)
        & ((to // 2) % 2 == (at // 2) % 2)
        & (to % 2 == at % 2)
    ).astype(BF16)
    onward_rows = pick(onward, middle).reshape(32, 16, 256)
    landed = lax.all_to_all(onward_rows, DP, 0, 0, tiled=True).reshape(512, 256)
    row = iota((ROWS, 512), 0)
    col = iota((ROWS, 512), 1)
    same = (
        ((row // 2) % 32 == col // 16) & (row // 64 == (col // 2) % 2) & (row % 2 == col % 2)
    )
    stream = jnp.concatenate(
        [pick((same & ((col // 4) % 4 == part)).astype(BF16), landed) for part in range(4)],
        axis=1,
    )

    kept = dropped == 0
    target = jnp.where(kept, (routes // 2) * CAP + bin_slots, -1)
    slot = iota((ROWS, 8, 32 * CAP), 2)

    def table(local, values):
        mine = jnp.where(routes % 2 == local, target, -1)
        hit = mine[:, :, None] == slot
        return jnp.sum(jnp.where(hit, values, 0.0), axis=1).astype(BF16)

    dispatch = [table(j, 1.0) for j in range(2)]
    combine = [table(j, route_weight[:, :, None]) for j in range(2)]

    def send_bins(j):
        rows = jnp.einsum("ib,ic->bc", dispatch[j], stream, preferred_element_type=F32)
        return lax.all_to_all(rows.astype(BF16).reshape(32, CAP, 1024), DP, 0, 0, tiled=True)

    def expert(j, blocks):
        squares = 0.0
        gate = 0.0
        up = 0.0
        for distance, block in enumerate(blocks):
            place = (x + distance) % 4
            wide = block.astype(F32)
            squares = squares + jnp.sum(wide * wide, axis=1, keepdims=True)
            gain = lax.dynamic_slice_in_dim(gains, place, 1, axis=0)
            scaled = (wide * gain).astype(BF16)
            gate_rows = lax.dynamic_slice_in_dim(gate_weight[j], place * 1024, 1024, axis=0)
            up_rows = lax.dynamic_slice_in_dim(up_weight[j], place * 1024, 1024, axis=0)
            gate = gate + jnp.dot(scaled, gate_rows, preferred_element_type=F32)
            up = up + jnp.dot(scaled, up_rows, preferred_element_type=F32)
        norm = lax.rsqrt(squares / D + 1e-6)
        return (jax.nn.silu(gate * norm) * (up * norm)).astype(BF16)

    def send_back(j, hidden):
        def down(distance):
            columns = lax.dynamic_slice_in_dim(
                down_weight[j], ((x + distance) % 4) * 1024, 1024, axis=1
            )
            return jnp.dot(hidden, columns, preferred_element_type=F32)

        one, two = ring_scatter(down(2).astype(BF16), down(1), down(3), "tensor")
        total = (down(0) + one.astype(F32) + two.astype(F32)).astype(BF16)
        return lax.all_to_all(total.reshape(32, CAP, 1024), DP, 0, 0, tiled=True)

    bins = [send_bins(j).reshape(32 * CAP, 1024) for j in range(2)]
    blocks = [ring_gather(b, "tensor") for b in bins]
    hidden = [expert(j, blocks[j]) for j in range(2)]
    back = [send_back(j, hidden[j]).reshape(32 * CAP, 1024) for j in range(2)]
    mix = sum(
        jnp.einsum("ib,bc->ic", combine[j], back[j], preferred_element_type=F32) for j in range(2)
    )
    return (stream, mix.astype(BF16))


def solution(mesh):
    fine = Mesh(mesh.devices.reshape(4, 4, 2, 4), ("y", "z", "core", "tensor"))
    return jax.shard_map(
        per_device,
        mesh=fine,
        in_specs=(
            P(DP, "tensor"),
            P(DP, "tensor"),
            P(DP, "tensor"),
            P(DP, "tensor"),
            P(),
            P(),
            P("tensor", DP),
            P("tensor"),
            P(DP, None),
            P(DP, None),
            P(DP, None),
            P(DP, None),
            P(DP, None, "tensor"),
            P(DP, None, "tensor"),
            P(DP, "tensor", None),
        ),
        out_specs=(P(DP, "tensor"), P(DP, "tensor")),
        check_vma=False,
    )
```

```python
import jax
import jax.numpy as jnp
from jax import lax
from jax.experimental import pallas as pl
from jax.experimental.pallas import tpu as pltpu
from jax.sharding import Mesh, PartitionSpec as P

D = 4096
HEAD_WIDTH = 128
PACK_ROWS = 64
QUERY_PER_KEY = 8
DP = ("y", "z", "core")
ROWS = 128
CAP = 16
BINS = 32 * CAP
PART = 1024
F32 = jnp.float32
BF16 = jnp.bfloat16

RIGHT = [(i, (i + 1) % 4) for i in range(4)]
LEFT = [(i, (i - 1) % 4) for i in range(4)]


def iota(shape, dim):
    return lax.broadcasted_iota(jnp.int32, shape, dim)


def whole(memory_space=pltpu.VMEM):
    return pl.BlockSpec(memory_space=memory_space)


def params(megabytes):
    return pltpu.CompilerParams(vmem_limit_bytes=megabytes << 20)


def after(values, *done):
    count = len(values)
    return pl.pallas_call(
        lambda *refs: None,
        out_shape=[jax.ShapeDtypeStruct(v.shape, v.dtype) for v in values],
        in_specs=[whole(pl.ANY)] * (count + len(done)),
        out_specs=[whole(pl.ANY)] * count,
        input_output_aliases={i: i for i in range(count)},
        name="after",
    )(*values, *done)


def attend_kernel(
    index, lengths, queries_in, keys_in, values_in, residual_in, out, queries, keys, values, residual, sems
):
    pairs = ((queries_in, queries), (keys_in, keys), (values_in, values), (residual_in, residual))
    copies = [pltpu.make_async_copy(a, b, sems.at[i]) for i, (a, b) in enumerate(pairs)]
    for copy in copies:
        copy.start()
    first = 2 * index[0]
    position = iota((ROWS, ROWS), 0)
    other = iota((ROWS, ROWS), 1)

    def label(at):
        second = at >= PACK_ROWS
        inner = jnp.where(second, at - PACK_ROWS, at)
        found = jnp.where(second, 8, 0)
        ends = [jnp.int32(0), jnp.int32(0)]
        for doc in range(4):
            for s in range(2):
                ends[s] = ends[s] + lengths[doc, first + s]
            found = found + (inner >= jnp.where(second, ends[1], ends[0])).astype(jnp.int32)
        return found

    hidden = jnp.where((label(position) == label(other)) & (position >= other), 0.0, -1e30)
    for copy in copies:
        copy.wait()
    lanes = [slice(h * HEAD_WIDTH, (h + 1) * HEAD_WIDTH) for h in range(QUERY_PER_KEY)]
    stacked = jnp.concatenate([queries[:, part] for part in lanes], axis=0)
    scores = lax.dot_general(
        stacked, keys[...], (((1,), (1,)), ((), ())), preferred_element_type=F32
    ).reshape(QUERY_PER_KEY, ROWS, ROWS)
    masked = jnp.where(hidden[None] < 0.0, -1e30, scores * HEAD_WIDTH**-0.5)
    exps = jnp.exp(masked - jnp.max(masked, axis=2, keepdims=True))
    probs = (exps / jnp.sum(exps, axis=2, keepdims=True)).astype(BF16)
    heads = jnp.dot(
        probs.reshape(QUERY_PER_KEY * ROWS, ROWS), values[...], preferred_element_type=F32
    )
    attended = jnp.concatenate(
        [heads[h * ROWS : (h + 1) * ROWS] for h in range(QUERY_PER_KEY)], axis=1
    )
    rest = residual[...].astype(F32)

    def group(rows, at):
        low = rows[at * 8 : at * 8 + 8]
        high = rows[PACK_ROWS + at * 8 : PACK_ROWS + at * 8 + 8]
        return jnp.concatenate([low, high], axis=0).astype(BF16)

    for y in range(4):
        for core in range(2):
            mine = group(attended, y * 2 + core)
            plain = group(rest, y * 2 + core)
            for z in range(4):
                out[y, z, core, :, :PART] = mine
                out[y, z, core, :, PART:] = plain[:, z * 256 : z * 256 + 256]


def route_kernel(plan, base, own, one, two, out, placed):
    total = own[...] + one[...].astype(F32) + two[...].astype(F32)
    merged = (base[...].astype(F32) + total).astype(BF16).astype(F32)
    for source in range(32):
        for s in range(2):
            rows = merged[source * 16 + s * 8 : source * 16 + s * 8 + 8]
            placed[plan[source * 2 + s], s * 8 : s * 8 + 8, :] = rows
    out[...] = placed[...].astype(BF16)


def stream_kernel(landed, table, stream, bins):
    parts = []
    for z in range(4):
        tiles = [landed[y, z, core].astype(F32) for y in range(4) for core in range(2)]
        parts.append(
            jnp.concatenate([t[s * 8 : s * 8 + 8] for s in range(2) for t in tiles], axis=0)
        )
    rows = jnp.concatenate(parts, axis=1).astype(BF16)
    stream[...] = rows
    bins[...] = jnp.dot(table[...], rows, preferred_element_type=F32).astype(BF16)


def tables_kernel(
    routes_t, slots_t, dropped_t, routes, slots, dropped, weight, send0, send1, mix0, mix1
):
    def target(named, slot, drop):
        return jnp.where(drop == 0, (named // 2) * CAP + slot, -1), named % 2

    across, side = target(routes_t[...], slots_t[...], dropped_t[...])
    row = iota((BINS, ROWS), 0)
    for local, out in enumerate((send0, send1)):
        mine = jnp.where(side == local, across, -1)
        total = jnp.zeros((BINS, ROWS), F32)
        for k in range(8):
            total = total + jnp.where(mine[k : k + 1] == row, 1.0, 0.0)
        out[...] = total.astype(BF16)
    down, side = target(routes[...], slots[...], dropped[...])
    column = iota((ROWS, BINS), 1)
    for local, out in enumerate((mix0, mix1)):
        mine = jnp.where(side == local, down, -1)
        total = jnp.zeros((ROWS, BINS), F32)
        for k in range(8):
            total = total + jnp.where(mine[:, k : k + 1] == column, weight[:, k : k + 1], 0.0)
        out[...] = total.astype(BF16)


def expert_kernel(
    index, own, right, left, top, low, gain, gate_w, up_w, down_w,
    far_top, far_low, right_top, right_low, left_top, left_low, own_out,
    rows, gate, up, squares, hidden, sems,
):
    step = pl.program_id(0)
    half = BINS // 2
    copies = [
        pltpu.make_async_copy(own, rows.at[0], sems.at[0]),
        pltpu.make_async_copy(right, rows.at[1], sems.at[1]),
        pltpu.make_async_copy(left, rows.at[2], sems.at[2]),
        pltpu.make_async_copy(top, rows.at[3, pl.ds(0, half)], sems.at[3]),
        pltpu.make_async_copy(low, rows.at[3, pl.ds(half, half)], sems.at[4]),
    ]

    @pl.when(step == 0)
    def _():
        for copy in copies:
            copy.start()
        gate[...] = jnp.zeros_like(gate)
        up[...] = jnp.zeros_like(up)
        squares[...] = jnp.zeros_like(squares)
        copies[0].wait()

    @pl.when(step == 1)
    def _():
        copies[1].wait()

    @pl.when(step == 2)
    def _():
        copies[2].wait()

    @pl.when(step == 3)
    def _():
        copies[3].wait()
        copies[4].wait()

    @pl.when(step < 4)
    def _():
        wide = rows[step].astype(F32)
        squares[...] += jnp.sum(wide * wide, axis=1, keepdims=True)
        scaled = (wide * gain[...]).astype(BF16)
        gate[...] += jnp.dot(scaled, gate_w[...], preferred_element_type=F32)
        up[...] += jnp.dot(scaled, up_w[...], preferred_element_type=F32)

    @pl.when(step == 3)
    def _():
        norm = lax.rsqrt(squares[...] * (1.0 / D) + 1e-6)
        gated = gate[...] * norm
        hidden[...] = (gated / (1.0 + jnp.exp(-gated)) * (up[...] * norm)).astype(BF16)

    @pl.when(step >= 4)
    def _():
        product = jnp.dot(hidden[...], down_w[...], preferred_element_type=F32).astype(BF16)

        @pl.when(step == 4)
        def _():
            far_top[...] = product[:half]
            far_low[...] = product[half:]

        @pl.when(step == 5)
        def _():
            left_top[...] = product[:half]
            left_low[...] = product[half:]

        @pl.when(step == 6)
        def _():
            right_top[...] = product[:half]
            right_low[...] = product[half:]

        @pl.when(step == 7)
        def _():
            own_out[...] = product


def ring_distance(step):
    return step ^ (step >> 1)


def run_expert(x, local, blocks, gains, gate_weight, up_weight, down_weight):
    def up_place(i, at):
        return (local, (at[0] + ring_distance(jnp.minimum(i, 3))) % 4, 0)

    def down_place(i, at):
        return (local, 0, (at[0] + ring_distance(7 - jnp.maximum(i, 4))) % 4)

    half = jax.ShapeDtypeStruct((BINS // 2, PART), BF16)
    grid = pltpu.PrefetchScalarGridSpec(
        num_scalar_prefetch=1,
        grid=(8,),
        in_specs=[whole(pl.ANY)] * 5
        + [
            pl.BlockSpec((None, 1, PART), lambda i, at: (jnp.minimum(i, 3), 0, 0)),
            pl.BlockSpec((None, PART, 384), up_place),
            pl.BlockSpec((None, PART, 384), up_place),
            pl.BlockSpec((None, 384, PART), down_place),
        ],
        out_specs=[pl.BlockSpec((BINS // 2, PART), lambda i, at: (0, 0))] * 6
        + [pl.BlockSpec((BINS, PART), lambda i, at: (0, 0))],
        scratch_shapes=[
            pltpu.VMEM((4, BINS, PART), BF16),
            pltpu.VMEM((BINS, 384), F32),
            pltpu.VMEM((BINS, 384), F32),
            pltpu.VMEM((BINS, 1), F32),
            pltpu.VMEM((BINS, 384), BF16),
            pltpu.SemaphoreType.DMA((5,)),
        ],
    )
    return pl.pallas_call(
        expert_kernel,
        grid_spec=grid,
        out_shape=[half] * 6 + [jax.ShapeDtypeStruct((BINS, PART), BF16)],
        compiler_params=params(40),
        cost_estimate=pl.CostEstimate(
            flops=6 * BINS * 4096 * 384, bytes_accessed=18 << 20, transcendentals=BINS * 384
        ),
        name="expert",
    )(x, *blocks, gains, gate_weight, up_weight, down_weight)


def ring_gather(block):
    half = block.shape[0] // 2
    left = lax.ppermute(block, "tensor", RIGHT)
    right = lax.ppermute(block, "tensor", LEFT)
    return (
        right,
        left,
        lax.ppermute(left[:half], "tensor", RIGHT),
        lax.ppermute(right[half:], "tensor", LEFT),
    )


def ring_scatter(far_top, far_low, right_top, right_low, left_top, left_low, plain_done=(), sum_done=()):
    if plain_done:
        far_top, far_low = after((far_top, far_low), *plain_done)
        right_low, left_top = after((right_low, left_top), *sum_done)
    top = lax.ppermute(far_top, "tensor", RIGHT)
    low = lax.ppermute(far_low, "tensor", LEFT)
    from_left_low = lax.ppermute(right_low, "tensor", RIGHT)
    from_right_top = lax.ppermute(left_top, "tensor", LEFT)
    right_sum = (right_top.astype(F32) + top.astype(F32)).astype(BF16)
    left_sum = (left_low.astype(F32) + low.astype(F32)).astype(BF16)
    from_left_top = lax.ppermute(right_sum, "tensor", RIGHT)
    from_right_low = lax.ppermute(left_sum, "tensor", LEFT)
    return from_left_top, from_left_low, from_right_top, from_right_low


def per_device(
    queries,
    rotated_key_rows,
    value_matrix,
    residual,
    lengths,
    move_plan,
    out_weight,
    norm_gain,
    routes,
    bin_slots,
    dropped,
    route_weight,
    gate_weight,
    up_weight,
    down_weight,
):
    x = lax.axis_index("tensor")
    d = lax.axis_index(DP)
    x_ref = jnp.reshape(x, (1,)).astype(jnp.int32)

    weight = lax.all_gather(out_weight, ("y", "core"), axis=1, tiled=True)

    sent = pl.pallas_call(
        attend_kernel,
        out_shape=jax.ShapeDtypeStruct((4, 4, 2, 16, PART + 256), BF16),
        in_specs=[whole(pltpu.SMEM)] * 2 + [whole(pl.ANY)] * 4,
        out_specs=whole(),
        scratch_shapes=[
            pltpu.VMEM((ROWS, PART), BF16),
            pltpu.VMEM((ROWS, HEAD_WIDTH), BF16),
            pltpu.VMEM((ROWS, HEAD_WIDTH), BF16),
            pltpu.VMEM((ROWS, PART), BF16),
            pltpu.SemaphoreType.DMA((4,)),
        ],
        compiler_params=params(24),
        name="attend",
    )(jnp.reshape(d, (1,)).astype(jnp.int32), lengths.T, queries, rotated_key_rows, value_matrix, residual)
    spread = lax.all_to_all(sent.reshape(32, 16, PART + 256), DP, 0, 0, tiled=True)
    spread = spread.reshape(512, PART + 256)

    send0, send1, mix0, mix1 = pl.pallas_call(
        tables_kernel,
        out_shape=[jax.ShapeDtypeStruct((BINS, ROWS), BF16)] * 2
        + [jax.ShapeDtypeStruct((ROWS, BINS), BF16)] * 2,
        in_specs=[whole()] * 7,
        out_specs=[whole()] * 4,
        compiler_params=params(24),
        name="tables",
    )(routes.T, bin_slots.T, dropped.T, routes, bin_slots, dropped, route_weight)
    own_gain = norm_gain.reshape(8, 128)
    right_gain, left_gain, top_gain, low_gain = ring_gather(own_gain)
    far_gain = jnp.concatenate([top_gain, low_gain], axis=0)
    gains = jnp.stack([own_gain, right_gain, left_gain, far_gain], axis=0).reshape(4, 1, PART)

    tokens = spread[:, :PART]

    def project(distance):
        columns = lax.dynamic_slice_in_dim(weight, ((x + distance) % 4) * 256, 256, axis=1)
        return jnp.dot(tokens, columns, preferred_element_type=F32)

    far = project(2).astype(BF16)
    right = project(1).astype(BF16)
    left = project(3).astype(BF16)
    a, b, c, e = ring_scatter(far[:256], far[256:], right[:256], right[256:], left[:256], left[256:])
    onward = pl.pallas_call(
        route_kernel,
        out_shape=jax.ShapeDtypeStruct((32, 16, 256), BF16),
        in_specs=[whole(pltpu.SMEM)] + [whole()] * 4,
        out_specs=whole(),
        scratch_shapes=[pltpu.VMEM((32, 16, 256), F32)],
        compiler_params=params(24),
        name="route",
    )(
        move_plan,
        spread[:, PART:],
        project(0),
        jnp.concatenate([a, b], axis=0),
        jnp.concatenate([c, e], axis=0),
    )
    landed = lax.all_to_all(onward, DP, 0, 0, tiled=True)

    stream, bins0 = pl.pallas_call(
        stream_kernel,
        out_shape=[
            jax.ShapeDtypeStruct((ROWS, PART), BF16),
            jax.ShapeDtypeStruct((BINS, PART), BF16),
        ],
        in_specs=[whole()] * 2,
        out_specs=[whole()] * 2,
        compiler_params=params(24),
        name="stream",
    )(landed.reshape(4, 4, 2, 16, 256), send0)
    bins1 = jnp.dot(send1, stream, preferred_element_type=F32).astype(BF16)

    def exchange(rows):
        return lax.all_to_all(rows.reshape(32, CAP, PART), DP, 0, 0, tiled=True).reshape(BINS, PART)

    held0 = exchange(bins0)
    near0 = ring_gather(held0)
    (held1,) = after((exchange(bins1),), near0[0], near0[1])
    near1 = ring_gather(held1)
    weights = (gate_weight, up_weight, down_weight)
    products0 = run_expert(x_ref, 0, (held0, *near0), gains, *weights)
    sums0 = ring_scatter(*products0[:6])
    products1 = run_expert(x_ref, 1, (held1, *near1), gains, *weights)
    sums1 = ring_scatter(*products1[:6], (sums0[1], sums0[2]), (sums0[0], sums0[3]))

    def total(own, a, b, c, e):
        arrived = jnp.concatenate([a.astype(F32) + c.astype(F32), b.astype(F32) + e.astype(F32)], axis=0)
        return (own.astype(F32) + arrived).astype(BF16)

    back = [exchange(total(products0[6], *sums0)), exchange(total(products1[6], *sums1))]
    mix = jnp.dot(mix0, back[0], preferred_element_type=F32)
    mix = mix + jnp.dot(mix1, back[1], preferred_element_type=F32)
    return (stream, mix.astype(BF16))


def solution(mesh):
    fine = Mesh(mesh.devices.reshape(4, 4, 2, 4), ("y", "z", "core", "tensor"))
    return jax.shard_map(
        per_device,
        mesh=fine,
        in_specs=(
            P(DP, "tensor"),
            P(DP, "tensor"),
            P(DP, "tensor"),
            P(DP, "tensor"),
            P(),
            P(),
            P("tensor", DP),
            P("tensor"),
            P(DP, None),
            P(DP, None),
            P(DP, None),
            P(DP, None),
            P(DP, None, "tensor"),
            P(DP, None, "tensor"),
            P(DP, "tensor", None),
        ),
        out_specs=(P(DP, "tensor"), P(DP, "tensor")),
        check_vma=False,
    )
```

```python
import functools

import jax
import jax.numpy as jnp
from jax import lax
from jax.experimental import pallas as pl
from jax.experimental.pallas import tpu as pltpu
from jax.sharding import Mesh, PartitionSpec as P

D = 4096
HEAD_WIDTH = 128
PACK_ROWS = 64
QUERY_PER_KEY = 8
DP = ("y", "z", "core")
ROWS = 128
CAP = 16
BINS = 32 * CAP
PART = 1024
VMEM = 60
UNITS = 384
F32 = jnp.float32
BF16 = jnp.bfloat16

RIGHT = [(i, (i + 1) % 4) for i in range(4)]
LEFT = [(i, (i - 1) % 4) for i in range(4)]


NO_COST = pl.CostEstimate(flops=0, bytes_accessed=0, transcendentals=0)


def iota(shape, dim):
    return lax.broadcasted_iota(jnp.int32, shape, dim)


def whole(memory_space=pltpu.VMEM):
    return pl.BlockSpec(memory_space=memory_space)


def params(megabytes):
    return pltpu.CompilerParams(vmem_limit_bytes=megabytes << 20)


def after(values, *done):
    count = len(values)
    return pl.pallas_call(
        lambda *refs: None,
        out_shape=[jax.ShapeDtypeStruct(v.shape, v.dtype) for v in values],
        in_specs=[whole(pltpu.HBM)] * (count + len(done)),
        out_specs=[whole(pltpu.HBM)] * count,
        input_output_aliases={i: i for i in range(count)},
        name="after",
    )(*values, *done)


def attend_kernel(
    index, lengths, queries_in, keys_in, values_in, residual_in, out, queries, keys, values, residual, sems
):
    pairs = ((queries_in, queries), (keys_in, keys), (values_in, values), (residual_in, residual))
    copies = [pltpu.make_async_copy(a, b, sems.at[i]) for i, (a, b) in enumerate(pairs)]
    for copy in copies:
        copy.start()
    first = 2 * index[0]
    position = iota((ROWS, ROWS), 0)
    other = iota((ROWS, ROWS), 1)

    def label(at):
        second = at >= PACK_ROWS
        inner = jnp.where(second, at - PACK_ROWS, at)
        found = jnp.where(second, 8, 0)
        ends = [jnp.int32(0), jnp.int32(0)]
        for doc in range(4):
            for s in range(2):
                ends[s] = ends[s] + lengths[doc, first + s]
            found = found + (inner >= jnp.where(second, ends[1], ends[0])).astype(jnp.int32)
        return found

    hidden = jnp.where((label(position) == label(other)) & (position >= other), 0.0, -1e30)
    for copy in copies:
        copy.wait()
    lanes = [slice(h * HEAD_WIDTH, (h + 1) * HEAD_WIDTH) for h in range(QUERY_PER_KEY)]
    stacked = jnp.concatenate([queries[:, part] for part in lanes], axis=0)
    scores = lax.dot_general(
        stacked, keys[...], (((1,), (1,)), ((), ())), preferred_element_type=F32
    ).reshape(QUERY_PER_KEY, ROWS, ROWS)
    masked = jnp.where(hidden[None] < 0.0, -1e30, scores * HEAD_WIDTH**-0.5)
    exps = jnp.exp(masked - jnp.max(masked, axis=2, keepdims=True))
    probs = (exps / jnp.sum(exps, axis=2, keepdims=True)).astype(BF16)
    heads = jnp.dot(
        probs.reshape(QUERY_PER_KEY * ROWS, ROWS), values[...], preferred_element_type=F32
    )
    attended = jnp.concatenate(
        [heads[h * ROWS : (h + 1) * ROWS] for h in range(QUERY_PER_KEY)], axis=1
    )
    rest = residual[...].astype(F32)

    def group(rows, at):
        low = rows[at * 8 : at * 8 + 8]
        high = rows[PACK_ROWS + at * 8 : PACK_ROWS + at * 8 + 8]
        return jnp.concatenate([low, high], axis=0).astype(BF16)

    for y in range(4):
        for core in range(2):
            mine = group(attended, y * 2 + core)
            plain = group(rest, y * 2 + core)
            for z in range(4):
                out[y, z, core, :, :PART] = mine
                out[y, z, core, :, PART:] = plain[:, z * 256 : z * 256 + 256]


def columns_kernel(distances, count, index, weight, gain, *rest):
    outs, sems = rest[-1 - len(distances) : -1], rest[-1]
    copies = []
    for n, (distance, first) in enumerate(distances):
        start = pl.multiple_of(((index[0] + distance) % 4) * PART, PART)
        for i in range(count):
            copies.append(
                pltpu.make_async_copy(
                    weight.at[first + i, :, pl.ds(start, PART)],
                    outs[n].at[pl.ds(i * UNITS, UNITS)],
                    sems.at[n * count + i],
                )
            )
    for copy in copies:
        copy.start()
    left = jnp.broadcast_to(gain[...], (16, PART))
    row = iota((16, PART), 0)
    terms = jnp.zeros((16, PART), F32)
    for k in range(3):
        term = left.astype(BF16).astype(F32)
        terms = jnp.where(row == k, term, terms)
        left = left - term
    for out in outs:
        out[pl.ds(count * UNITS, 16), :] = terms.astype(BF16)
    for copy in copies:
        copy.wait()


def run_columns(x, weight, gain, distances, count, *done):
    rows = count * UNITS + 16
    return pl.pallas_call(
        functools.partial(columns_kernel, distances, count),
        out_shape=[jax.ShapeDtypeStruct((rows, PART), BF16)] * len(distances),
        in_specs=[whole(pltpu.SMEM), whole(pltpu.HBM), whole()] + [whole(pltpu.HBM)] * len(done),
        out_specs=[whole()] * len(distances),
        scratch_shapes=[pltpu.SemaphoreType.DMA((len(distances) * count,))],
        compiler_params=params(VMEM),
        cost_estimate=NO_COST,
        name="columns",
    )(x, weight, gain, *done)


def project_kernel(
    index, rows, weight, far_top, far_low, right_top, right_low, left_top, left_low, mine
):
    def product(distance):
        start = pl.multiple_of(((index[0] + distance) % 4) * 256, 256)
        return jnp.dot(rows[:, :PART], weight[:, pl.ds(start, 256)], preferred_element_type=F32)

    for distance, upper, lower in ((2, far_top, far_low), (1, right_top, right_low), (3, left_top, left_low)):
        result = product(distance).astype(BF16)
        upper[...] = result[:256]
        lower[...] = result[256:]
    mine[...] = product(0) + rows[:, PART:].astype(F32)


def route_kernel(plan, own, one_top, one_low, two_top, two_low, out, placed):
    top = own[:256] + (one_top[...].astype(F32) + two_top[...].astype(F32))
    low = own[256:] + (one_low[...].astype(F32) + two_low[...].astype(F32))
    for source in range(32):
        at = source * 16
        half = top[at : at + 16] if at < 256 else low[at - 256 : at - 240]
        merged = half.astype(BF16).astype(F32)
        for s in range(2):
            placed[plan[source * 2 + s], s * 8 : s * 8 + 8, :] = merged[s * 8 : s * 8 + 8]
    out[...] = placed[...].astype(BF16)


def stream_kernel(landed, table, stream, bins):
    parts = []
    for z in range(4):
        tiles = [landed[y, z, core].astype(F32) for y in range(4) for core in range(2)]
        parts.append(
            jnp.concatenate([t[s * 8 : s * 8 + 8] for s in range(2) for t in tiles], axis=0)
        )
    rows = jnp.concatenate(parts, axis=1).astype(BF16)
    stream[...] = rows
    bins[...] = jnp.dot(table[...], rows, preferred_element_type=F32).astype(BF16)


def tables_kernel(
    routes_t, slots_t, dropped_t, routes, slots, dropped, weight, send0, send1, mix
):
    across = jnp.where(dropped_t[...] == 0, (routes_t[...] // 2) * CAP + slots_t[...], -1)
    row = iota((BINS, ROWS), 0)
    for local, out in enumerate((send0, send1)):
        mine = jnp.where(routes_t[...] % 2 == local, across, -1)
        total = jnp.zeros((BINS, ROWS), F32)
        for k in range(8):
            total = total + jnp.where(mine[k : k + 1] == row, 1.0, 0.0)
        out[...] = total.astype(BF16)
    down = jnp.where(dropped[...] == 0, routes[...] * CAP + slots[...], -1)
    column = iota((ROWS, 2 * BINS), 1)
    total = jnp.zeros((ROWS, 2 * BINS), F32)
    for k in range(8):
        total = total + jnp.where(down[:, k : k + 1] == column, weight[:, k : k + 1], 0.0)
    mix[...] = total.astype(BF16)


def near_kernel(index, own, right, left, gain, gate_w, up_w, total, squares, rows, sems):
    step = pl.program_id(0)
    copies = [
        pltpu.make_async_copy(source, rows.at[i], sems.at[i])
        for i, source in enumerate((own, right, left))
    ]

    @pl.when(step == 0)
    def _():
        for copy in copies:
            copy.start()
        total[...] = jnp.zeros_like(total)
        squares[...] = jnp.zeros_like(squares)
        copies[0].wait()

    @pl.when(step == 1)
    def _():
        copies[1].wait()

    @pl.when(step == 2)
    def _():
        copies[2].wait()

    wide = rows[step].astype(F32)
    squares[...] += jnp.sum(wide * wide, axis=1, keepdims=True)
    scaled = (wide * gain[...]).astype(BF16)
    both = jnp.concatenate([gate_w[...], up_w[...]], axis=1)
    total[...] += jnp.dot(scaled, both, preferred_element_type=F32)


def far_kernel(index, top, low, total, squares, gain, gate_w, up_w, hidden):
    wide = jnp.concatenate([top[...], low[...]], axis=0).astype(F32)
    mean = (squares[...] + jnp.sum(wide * wide, axis=1, keepdims=True)) * (1.0 / D)
    norm = lax.rsqrt(mean + 1e-6)
    scaled = (wide * gain[...]).astype(BF16)
    both = jnp.concatenate([gate_w[...], up_w[...]], axis=1)
    values = (total[...] + jnp.dot(scaled, both, preferred_element_type=F32)) * norm
    gate = values[:, :UNITS]
    hidden[...] = (gate / (1.0 + jnp.exp(-gate)) * values[:, UNITS:]).astype(BF16)


def flat(shape):
    return pl.BlockSpec(shape, lambda i, at: (0, 0))


def gain_at(slot):
    return pl.BlockSpec((None, 1, PART), lambda i, at: (slot(i), 0, 0))


def weights_at(local, place):
    return [pl.BlockSpec((None, PART, UNITS), lambda i, at: (local, place(i, at), 0))] * 2


def run_near(x, local, blocks, gains, gate_weight, up_weight):
    return pl.pallas_call(
        near_kernel,
        grid_spec=pltpu.PrefetchScalarGridSpec(
            num_scalar_prefetch=1,
            grid=(3,),
            in_specs=[whole(pltpu.HBM)] * 3
            + [gain_at(lambda i: i)]
            + weights_at(local, lambda i, at: (at[0] + (i ^ (i >> 1))) % 4),
            out_specs=[flat((BINS, 2 * UNITS)), flat((BINS, 1))],
            scratch_shapes=[pltpu.VMEM((3, BINS, PART), BF16), pltpu.SemaphoreType.DMA((3,))],
        ),
        out_shape=[
            jax.ShapeDtypeStruct((BINS, 2 * UNITS), F32),
            jax.ShapeDtypeStruct((BINS, 1), F32),
        ],
        compiler_params=params(VMEM),
        cost_estimate=NO_COST,
        name="near",
    )(x, *blocks, gains, gate_weight, up_weight)


def run_far(x, local, blocks, near, gains, gate_weight, up_weight):
    return pl.pallas_call(
        far_kernel,
        grid_spec=pltpu.PrefetchScalarGridSpec(
            num_scalar_prefetch=1,
            grid=(1,),
            in_specs=[flat(v.shape) for v in (*blocks, *near)]
            + [gain_at(lambda i: 3)]
            + weights_at(local, lambda i, at: (at[0] + 2) % 4),
            out_specs=flat((BINS, UNITS)),
        ),
        out_shape=jax.ShapeDtypeStruct((BINS, UNITS), BF16),
        compiler_params=params(VMEM),
        cost_estimate=NO_COST,
        name="far",
    )(x, *blocks, *near, gains, gate_weight, up_weight)


def down_kernel(
    local, index, own, right, left, top, low, own_w, right_w, left_w, far_w, *rest
):
    out, units, weights, product, sems = rest[-5:]
    half = BINS // 2
    column = pl.multiple_of(index[0] * PART, PART)
    rows = pl.ds(local * UNITS, UNITS)
    pairs = (
        (own, units.at[0]),
        (own_w.at[local, :, pl.ds(column, PART)], weights.at[0]),
        (right, units.at[1]),
        (right_w.at[rows], weights.at[1]),
        (left, units.at[2]),
        (left_w.at[rows], weights.at[2]),
        (top, units.at[3, pl.ds(0, half)]),
        (low, units.at[3, pl.ds(half, half)]),
        (far_w.at[pl.ds(0, UNITS)], weights.at[3]),
    )
    copies = [pltpu.make_async_copy(a, b, sems.at[i]) for i, (a, b) in enumerate(pairs)]
    for copy in copies:
        copy.start()
    total = 0.0
    for block in range(4):
        for copy in copies[2 * block : 2 * block + (3 if block == 3 else 2)]:
            copy.wait()
        total = total + jnp.dot(units[block], weights[block], preferred_element_type=F32)
    product[...] = total.astype(BF16).reshape(32, CAP, PART)
    result = pltpu.make_async_copy(product, out.at[:, local], sems.at[9])
    result.start()
    result.wait()


def run_down(x, local, blocks, down_weight, right_w, left_w, far_w, *more, into=None):
    given = (*blocks, down_weight, right_w, left_w, far_w, *more) + (() if into is None else (into,))
    return pl.pallas_call(
        functools.partial(down_kernel, local),
        out_shape=jax.ShapeDtypeStruct((32, 2, CAP, PART), BF16),
        in_specs=[whole(pltpu.SMEM)] + [whole(pl.ANY)] * len(given),
        out_specs=whole(pltpu.HBM),
        input_output_aliases={} if into is None else {len(given): 0},
        scratch_shapes=[
            pltpu.VMEM((4, BINS, UNITS), BF16),
            pltpu.VMEM((4, UNITS, PART), BF16),
            pltpu.VMEM((32, CAP, PART), BF16),
            pltpu.SemaphoreType.DMA((10,)),
        ],
        compiler_params=params(VMEM),
        cost_estimate=NO_COST,
        name="down",
    )(x, *given)


def ring_gather(block, axis="tensor", done=()):
    half = block.shape[0] // 2
    left = lax.ppermute(block, axis, RIGHT)
    right = lax.ppermute(block, axis, LEFT)
    upper, lower = left[:half], right[half:]
    if done:
        upper, lower = after((upper, lower), *done)
    return right, left, lax.ppermute(upper, axis, RIGHT), lax.ppermute(lower, axis, LEFT)


def ring_scatter(far_top, far_low, right_top, right_low, left_top, left_low):
    top = lax.ppermute(far_top, "tensor", RIGHT)
    low = lax.ppermute(far_low, "tensor", LEFT)
    from_left_low = lax.ppermute(right_low, "tensor", RIGHT)
    from_right_top = lax.ppermute(left_top, "tensor", LEFT)
    right_sum = (right_top.astype(F32) + top.astype(F32)).astype(BF16)
    left_sum = (left_low.astype(F32) + low.astype(F32)).astype(BF16)
    from_left_top = lax.ppermute(right_sum, "tensor", RIGHT)
    from_right_low = lax.ppermute(left_sum, "tensor", LEFT)
    return from_left_top, from_left_low, from_right_top, from_right_low


def per_device(
    queries,
    rotated_key_rows,
    value_matrix,
    residual,
    lengths,
    move_plan,
    out_weight,
    norm_gain,
    routes,
    bin_slots,
    dropped,
    route_weight,
    gate_weight,
    up_weight,
    down_weight,
):
    x = lax.axis_index("tensor")
    d = lax.axis_index(DP)
    x_ref = jnp.reshape(x, (1,)).astype(jnp.int32)

    weight = lax.all_gather(out_weight, ("y", "core"), axis=1, tiled=True)

    sent = pl.pallas_call(
        attend_kernel,
        out_shape=jax.ShapeDtypeStruct((4, 4, 2, 16, PART + 256), BF16),
        in_specs=[whole(pltpu.SMEM)] * 2 + [whole(pl.ANY)] * 4,
        out_specs=whole(),
        scratch_shapes=[
            pltpu.VMEM((ROWS, PART), BF16),
            pltpu.VMEM((ROWS, HEAD_WIDTH), BF16),
            pltpu.VMEM((ROWS, HEAD_WIDTH), BF16),
            pltpu.VMEM((ROWS, PART), BF16),
            pltpu.SemaphoreType.DMA((4,)),
        ],
        compiler_params=params(VMEM),
        cost_estimate=NO_COST,
        name="attend",
    )(jnp.reshape(d, (1,)).astype(jnp.int32), lengths.T, queries, rotated_key_rows, value_matrix, residual)
    spread = lax.all_to_all(sent.reshape(32, 16, PART + 256), DP, 0, 0, tiled=True)
    spread = spread.reshape(512, PART + 256)

    send0, send1, mix = pl.pallas_call(
        tables_kernel,
        out_shape=[jax.ShapeDtypeStruct((BINS, ROWS), BF16)] * 2
        + [jax.ShapeDtypeStruct((ROWS, 2 * BINS), BF16)],
        in_specs=[whole()] * 7,
        out_specs=[whole()] * 3,
        compiler_params=params(VMEM),
        cost_estimate=NO_COST,
        name="tables",
    )(routes.T, bin_slots.T, dropped.T, routes, bin_slots, dropped, route_weight)
    own_gain = norm_gain.reshape(1, PART)
    for_right, for_left = run_columns(x_ref, down_weight, own_gain, ((1, 0), (3, 0)), 2)
    left_w = lax.ppermute(for_right, "tensor", RIGHT)
    right_w = lax.ppermute(for_left, "tensor", LEFT)
    far0, far1 = run_columns(x_ref, down_weight, own_gain, ((2, 0), (2, 1)), 1, sent)
    (weight,) = after((weight,), left_w, right_w, far0, far1, send0)

    half = jax.ShapeDtypeStruct((256, 256), BF16)
    *partial, mine = pl.pallas_call(
        project_kernel,
        out_shape=[half] * 6 + [jax.ShapeDtypeStruct((512, 256), F32)],
        in_specs=[whole(pltpu.SMEM)] + [whole()] * 2,
        out_specs=[whole()] * 7,
        compiler_params=params(VMEM),
        cost_estimate=NO_COST,
        name="project",
    )(x_ref, spread, weight)
    sums = ring_scatter(*partial)
    onward = pl.pallas_call(
        route_kernel,
        out_shape=jax.ShapeDtypeStruct((32, 16, 256), BF16),
        in_specs=[whole(pltpu.SMEM)] + [whole()] * 5,
        out_specs=whole(),
        scratch_shapes=[pltpu.VMEM((32, 16, 256), F32)],
        compiler_params=params(VMEM),
        cost_estimate=NO_COST,
        name="route",
    )(move_plan, mine, *sums)
    landed = lax.all_to_all(onward, DP, 0, 0, tiled=True)
    far0, far1 = after((far0, far1), onward)
    far_w0 = lax.ppermute(far0, "tensor", RIGHT)
    far_w1 = lax.ppermute(far1, "tensor", LEFT)
    far_w0 = lax.ppermute(far_w0, "tensor", RIGHT)
    far_w1 = lax.ppermute(far_w1, "tensor", LEFT)

    stream, bins0 = pl.pallas_call(
        stream_kernel,
        out_shape=[
            jax.ShapeDtypeStruct((ROWS, PART), BF16),
            jax.ShapeDtypeStruct((BINS, PART), BF16),
        ],
        in_specs=[whole()] * 2,
        out_specs=[whole()] * 2,
        compiler_params=params(VMEM),
        cost_estimate=NO_COST,
        name="stream",
    )(landed.reshape(4, 4, 2, 16, 256), send0)
    bins1 = jnp.dot(send1, stream, preferred_element_type=F32).astype(BF16)

    def exchange(rows):
        return lax.all_to_all(rows.reshape(32, CAP, PART), DP, 0, 0, tiled=True).reshape(BINS, PART)

    held0 = exchange(bins0)
    (bins1,) = after((bins1,), far_w0, far_w1)

    def whole_gain(rows):
        return jnp.sum(rows[-16:].astype(F32), axis=0, keepdims=True)

    gains = jnp.stack([own_gain, whole_gain(right_w), whole_gain(left_w), whole_gain(far_w0)], axis=0)
    weights = (gate_weight, up_weight)
    right0, left0, top0, low0 = ring_gather(held0)
    partial0 = run_near(x_ref, 0, (held0, right0, left0), gains, *weights)
    (held1,) = after((exchange(bins1),), top0, low0, partial0[1])
    hidden0 = run_far(x_ref, 0, (top0, low0), partial0, gains, *weights)
    units0 = ring_gather(hidden0)
    right1, left1, top1, low1 = ring_gather(held1, done=units0[:2])
    partial1 = run_near(x_ref, 1, (held1, right1, left1), gains, *weights)
    hidden1 = run_far(x_ref, 1, (top1, low1), partial1, gains, *weights)
    units1 = ring_gather(hidden1)
    back = run_down(x_ref, 0, (hidden0, *units0), down_weight, right_w, left_w, far_w0, hidden1)
    back = run_down(x_ref, 1, (hidden1, *units1), down_weight, right_w, left_w, far_w1, into=back)
    back = lax.all_to_all(back.reshape(32, 2 * CAP, PART), DP, 0, 0, tiled=True)
    result = jnp.dot(mix, back.reshape(2 * BINS, PART), preferred_element_type=F32)
    return (stream, result.astype(BF16))


def solution(mesh):
    fine = Mesh(mesh.devices.reshape(4, 4, 2, 4), ("y", "z", "core", "tensor"))
    return jax.shard_map(
        per_device,
        mesh=fine,
        in_specs=(
            P(DP, "tensor"),
            P(DP, "tensor"),
            P(DP, "tensor"),
            P(DP, "tensor"),
            P(),
            P(),
            P("tensor", DP),
            P("tensor"),
            P(DP, None),
            P(DP, None),
            P(DP, None),
            P(DP, None),
            P(DP, None, "tensor"),
            P(DP, None, "tensor"),
            P(DP, "tensor", None),
        ),
        out_specs=(P(DP, "tensor"), P(DP, "tensor")),
        check_vma=False,
    )
```

```python
import functools

import jax
import jax.numpy as jnp
from jax import lax
from jax.experimental import pallas as pl
from jax.experimental.pallas import tpu as pltpu
from jax.sharding import Mesh, PartitionSpec as P

D = 4096
HEAD_WIDTH = 128
PACK_ROWS = 64
QUERY_PER_KEY = 8
DP = ("y", "z", "core")
ROWS = 128
CAP = 16
BINS = 32 * CAP
PART = 1024
VMEM = 60
UNITS = 384
F32 = jnp.float32
BF16 = jnp.bfloat16

RIGHT = [(i, (i + 1) % 4) for i in range(4)]
LEFT = [(i, (i - 1) % 4) for i in range(4)]


NO_COST = pl.CostEstimate(flops=0, bytes_accessed=0, transcendentals=0)


def iota(shape, dim):
    return lax.broadcasted_iota(jnp.int32, shape, dim)


def whole(memory_space=pltpu.VMEM):
    return pl.BlockSpec(memory_space=memory_space)


def params(megabytes):
    return pltpu.CompilerParams(vmem_limit_bytes=megabytes << 20)


def after(values, *done):
    count = len(values)
    return pl.pallas_call(
        lambda *refs: None,
        out_shape=[jax.ShapeDtypeStruct(v.shape, v.dtype) for v in values],
        in_specs=[whole(pltpu.HBM)] * (count + len(done)),
        out_specs=[whole(pltpu.HBM)] * count,
        input_output_aliases={i: i for i in range(count)},
        name="after",
    )(*values, *done)


def attend_kernel(
    index, lengths, queries_in, keys_in, values_in, residual_in, out, queries, keys, values, residual, sems
):
    pairs = ((queries_in, queries), (keys_in, keys), (values_in, values), (residual_in, residual))
    copies = [pltpu.make_async_copy(a, b, sems.at[i]) for i, (a, b) in enumerate(pairs)]
    for copy in copies:
        copy.start()
    first = 2 * index[0]
    position = iota((ROWS, ROWS), 0)
    other = iota((ROWS, ROWS), 1)

    def label(at):
        second = at >= PACK_ROWS
        inner = jnp.where(second, at - PACK_ROWS, at)
        found = jnp.where(second, 8, 0)
        ends = [jnp.int32(0), jnp.int32(0)]
        for doc in range(4):
            for s in range(2):
                ends[s] = ends[s] + lengths[doc, first + s]
            found = found + (inner >= jnp.where(second, ends[1], ends[0])).astype(jnp.int32)
        return found

    hidden = jnp.where((label(position) == label(other)) & (position >= other), 0.0, -1e30)
    for copy in copies:
        copy.wait()
    lanes = [slice(h * HEAD_WIDTH, (h + 1) * HEAD_WIDTH) for h in range(QUERY_PER_KEY)]
    stacked = jnp.concatenate([queries[:, part] for part in lanes], axis=0)
    scores = lax.dot_general(
        stacked, keys[...], (((1,), (1,)), ((), ())), preferred_element_type=F32
    ).reshape(QUERY_PER_KEY, ROWS, ROWS)
    masked = jnp.where(hidden[None] < 0.0, -1e30, scores * HEAD_WIDTH**-0.5)
    exps = jnp.exp(masked - jnp.max(masked, axis=2, keepdims=True))
    probs = (exps / jnp.sum(exps, axis=2, keepdims=True)).astype(BF16)
    heads = jnp.dot(
        probs.reshape(QUERY_PER_KEY * ROWS, ROWS), values[...], preferred_element_type=F32
    )
    attended = jnp.concatenate(
        [heads[h * ROWS : (h + 1) * ROWS] for h in range(QUERY_PER_KEY)], axis=1
    )
    rest = residual[...].astype(F32)

    def group(rows, at):
        low = rows[at * 8 : at * 8 + 8]
        high = rows[PACK_ROWS + at * 8 : PACK_ROWS + at * 8 + 8]
        return jnp.concatenate([low, high], axis=0).astype(BF16)

    for y in range(4):
        for core in range(2):
            mine = group(attended, y * 2 + core)
            plain = group(rest, y * 2 + core)
            for z in range(4):
                out[y, z, core, :, :PART] = mine
                out[y, z, core, :, PART:] = plain[:, z * 256 : z * 256 + 256]


def columns_kernel(distances, count, index, weight, gain, *rest):
    outs, sems = rest[-1 - len(distances) : -1], rest[-1]
    copies = []
    for n, (distance, first) in enumerate(distances):
        start = pl.multiple_of(((index[0] + distance) % 4) * PART, PART)
        for i in range(count):
            copies.append(
                pltpu.make_async_copy(
                    weight.at[first + i, :, pl.ds(start, PART)],
                    outs[n].at[pl.ds(i * UNITS, UNITS)],
                    sems.at[n * count + i],
                )
            )
    for copy in copies:
        copy.start()
    left = jnp.broadcast_to(gain[...], (16, PART))
    row = iota((16, PART), 0)
    terms = jnp.zeros((16, PART), F32)
    for k in range(3):
        term = left.astype(BF16).astype(F32)
        terms = jnp.where(row == k, term, terms)
        left = left - term
    for out in outs:
        out[pl.ds(count * UNITS, 16), :] = terms.astype(BF16)
    for copy in copies:
        copy.wait()


def run_columns(x, weight, gain, distances, count, *done):
    rows = count * UNITS + 16
    return pl.pallas_call(
        functools.partial(columns_kernel, distances, count),
        out_shape=[jax.ShapeDtypeStruct((rows, PART), BF16)] * len(distances),
        in_specs=[whole(pltpu.SMEM), whole(pltpu.HBM), whole()] + [whole(pltpu.HBM)] * len(done),
        out_specs=[whole()] * len(distances),
        scratch_shapes=[pltpu.SemaphoreType.DMA((len(distances) * count,))],
        compiler_params=params(VMEM),
        cost_estimate=NO_COST,
        name="columns",
    )(x, weight, gain, *done)


def project_kernel(
    index, rows, weight, far_top, far_low, right_top, right_low, left_top, left_low, mine
):
    def product(distance):
        first = ((index[0] + distance) % 4) * 2
        columns = jnp.concatenate([weight[first], weight[first + 1]], axis=1)
        return jnp.dot(rows[:, :PART], columns, preferred_element_type=F32)

    for distance, upper, lower in ((2, far_top, far_low), (1, right_top, right_low), (3, left_top, left_low)):
        result = product(distance).astype(BF16)
        upper[...] = result[:256]
        lower[...] = result[256:]
    mine[...] = product(0) + rows[:, PART:].astype(F32)


def route_kernel(plan, own, one_top, one_low, two_top, two_low, out, placed):
    top = own[:256] + (one_top[...].astype(F32) + two_top[...].astype(F32))
    low = own[256:] + (one_low[...].astype(F32) + two_low[...].astype(F32))
    for source in range(32):
        at = source * 16
        half = top[at : at + 16] if at < 256 else low[at - 256 : at - 240]
        merged = half.astype(BF16).astype(F32)
        for s in range(2):
            placed[plan[source * 2 + s], s * 8 : s * 8 + 8, :] = merged[s * 8 : s * 8 + 8]
    out[...] = placed[...].astype(BF16)


def stream_kernel(landed, table, stream, bins):
    parts = []
    for z in range(4):
        tiles = [landed[y, z, core].astype(F32) for y in range(4) for core in range(2)]
        parts.append(
            jnp.concatenate([t[s * 8 : s * 8 + 8] for s in range(2) for t in tiles], axis=0)
        )
    rows = jnp.concatenate(parts, axis=1).astype(BF16)
    stream[...] = rows
    bins[...] = jnp.dot(table[...], rows, preferred_element_type=F32).astype(BF16)


def tables_kernel(
    routes_t, slots_t, dropped_t, routes, slots, dropped, weight, send0, send1, mix
):
    across = jnp.where(dropped_t[...] == 0, (routes_t[...] // 2) * CAP + slots_t[...], -1)
    row = iota((BINS, ROWS), 0)
    for local, out in enumerate((send0, send1)):
        mine = jnp.where(routes_t[...] % 2 == local, across, -1)
        total = jnp.zeros((BINS, ROWS), F32)
        for k in range(8):
            total = total + jnp.where(mine[k : k + 1] == row, 1.0, 0.0)
        out[...] = total.astype(BF16)
    down = jnp.where(dropped[...] == 0, routes[...] * CAP + slots[...], -1)
    column = iota((ROWS, 2 * BINS), 1)
    total = jnp.zeros((ROWS, 2 * BINS), F32)
    for k in range(8):
        total = total + jnp.where(down[:, k : k + 1] == column, weight[:, k : k + 1], 0.0)
    mix[...] = total.astype(BF16)


def near_kernel(index, own, right, left, gain, gate_w, up_w, total, squares, rows, sems):
    step = pl.program_id(0)
    copies = [
        pltpu.make_async_copy(source, rows.at[i], sems.at[i])
        for i, source in enumerate((own, right, left))
    ]

    @pl.when(step == 0)
    def _():
        for copy in copies:
            copy.start()
        total[...] = jnp.zeros_like(total)
        squares[...] = jnp.zeros_like(squares)
        copies[0].wait()

    @pl.when(step == 1)
    def _():
        copies[1].wait()

    @pl.when(step == 2)
    def _():
        copies[2].wait()

    wide = rows[step].astype(F32)
    squares[...] += jnp.sum(wide * wide, axis=1, keepdims=True)
    scaled = (wide * gain[...]).astype(BF16)
    both = jnp.concatenate([gate_w[...], up_w[...]], axis=1)
    total[...] += jnp.dot(scaled, both, preferred_element_type=F32)


def far_kernel(index, top, low, total, squares, gain, gate_w, up_w, hidden):
    wide = jnp.concatenate([top[...], low[...]], axis=0).astype(F32)
    mean = (squares[...] + jnp.sum(wide * wide, axis=1, keepdims=True)) * (1.0 / D)
    norm = lax.rsqrt(mean + 1e-6)
    scaled = (wide * gain[...]).astype(BF16)
    both = jnp.concatenate([gate_w[...], up_w[...]], axis=1)
    values = (total[...] + jnp.dot(scaled, both, preferred_element_type=F32)) * norm
    gate = values[:, :UNITS]
    hidden[...] = (gate / (1.0 + jnp.exp(-gate)) * values[:, UNITS:]).astype(BF16)


def flat(shape):
    return pl.BlockSpec(shape, lambda i, at: (0, 0))


def gain_at(slot):
    return pl.BlockSpec((None, 1, PART), lambda i, at: (slot(i), 0, 0))


def weights_at(local, place):
    return [pl.BlockSpec((None, PART, UNITS), lambda i, at: (local, place(i, at), 0))] * 2


def run_near(x, local, blocks, gains, gate_weight, up_weight):
    return pl.pallas_call(
        near_kernel,
        grid_spec=pltpu.PrefetchScalarGridSpec(
            num_scalar_prefetch=1,
            grid=(3,),
            in_specs=[whole(pltpu.HBM)] * 3
            + [gain_at(lambda i: i)]
            + weights_at(local, lambda i, at: (at[0] + (i ^ (i >> 1))) % 4),
            out_specs=[flat((BINS, 2 * UNITS)), flat((BINS, 1))],
            scratch_shapes=[pltpu.VMEM((3, BINS, PART), BF16), pltpu.SemaphoreType.DMA((3,))],
        ),
        out_shape=[
            jax.ShapeDtypeStruct((BINS, 2 * UNITS), F32),
            jax.ShapeDtypeStruct((BINS, 1), F32),
        ],
        compiler_params=params(VMEM),
        cost_estimate=NO_COST,
        name="near",
    )(x, *blocks, gains, gate_weight, up_weight)


def run_far(x, local, blocks, near, gains, gate_weight, up_weight):
    return pl.pallas_call(
        far_kernel,
        grid_spec=pltpu.PrefetchScalarGridSpec(
            num_scalar_prefetch=1,
            grid=(1,),
            in_specs=[flat(v.shape) for v in (*blocks, *near)]
            + [gain_at(lambda i: 3)]
            + weights_at(local, lambda i, at: (at[0] + 2) % 4),
            out_specs=flat((BINS, UNITS)),
        ),
        out_shape=jax.ShapeDtypeStruct((BINS, UNITS), BF16),
        compiler_params=params(VMEM),
        cost_estimate=NO_COST,
        name="far",
    )(x, *blocks, *near, gains, gate_weight, up_weight)


def down_kernel(
    local, index, own, right, left, top, low, own_w, right_w, left_w, far_w, *rest
):
    out, units, weights, product, sems = rest[-5:]
    half = BINS // 2
    column = pl.multiple_of(index[0] * PART, PART)
    rows = pl.ds(local * UNITS, UNITS)
    pairs = (
        (own, units.at[0]),
        (own_w.at[local, :, pl.ds(column, PART)], weights.at[0]),
        (right, units.at[1]),
        (right_w.at[rows], weights.at[1]),
        (left, units.at[2]),
        (left_w.at[rows], weights.at[2]),
        (top, units.at[3, pl.ds(0, half)]),
        (low, units.at[3, pl.ds(half, half)]),
        (far_w.at[pl.ds(0, UNITS)], weights.at[3]),
    )
    copies = [pltpu.make_async_copy(a, b, sems.at[i]) for i, (a, b) in enumerate(pairs)]
    for copy in copies:
        copy.start()
    total = 0.0
    for block in range(4):
        for copy in copies[2 * block : 2 * block + (3 if block == 3 else 2)]:
            copy.wait()
        total = total + jnp.dot(units[block], weights[block], preferred_element_type=F32)
    product[...] = total.astype(BF16).reshape(32, CAP, PART)
    result = pltpu.make_async_copy(product, out.at[:, local], sems.at[9])
    result.start()
    result.wait()


def run_down(x, local, blocks, down_weight, right_w, left_w, far_w, *more, into=None):
    given = (*blocks, down_weight, right_w, left_w, far_w, *more) + (() if into is None else (into,))
    return pl.pallas_call(
        functools.partial(down_kernel, local),
        out_shape=jax.ShapeDtypeStruct((32, 2, CAP, PART), BF16),
        in_specs=[whole(pltpu.SMEM)] + [whole(pl.ANY)] * len(given),
        out_specs=whole(pltpu.HBM),
        input_output_aliases={} if into is None else {len(given): 0},
        scratch_shapes=[
            pltpu.VMEM((4, BINS, UNITS), BF16),
            pltpu.VMEM((4, UNITS, PART), BF16),
            pltpu.VMEM((32, CAP, PART), BF16),
            pltpu.SemaphoreType.DMA((10,)),
        ],
        compiler_params=params(VMEM),
        cost_estimate=NO_COST,
        name="down",
    )(x, *given)


def ring_gather(block, axis="tensor", done=()):
    half = block.shape[0] // 2
    left = lax.ppermute(block, axis, RIGHT)
    right = lax.ppermute(block, axis, LEFT)
    upper, lower = left[:half], right[half:]
    if done:
        upper, lower = after((upper, lower), *done)
    return right, left, lax.ppermute(upper, axis, RIGHT), lax.ppermute(lower, axis, LEFT)


def ring_scatter(far_top, far_low, right_top, right_low, left_top, left_low):
    top = lax.ppermute(far_top, "tensor", RIGHT)
    low = lax.ppermute(far_low, "tensor", LEFT)
    from_left_low = lax.ppermute(right_low, "tensor", RIGHT)
    from_right_top = lax.ppermute(left_top, "tensor", LEFT)
    right_sum = (right_top.astype(F32) + top.astype(F32)).astype(BF16)
    left_sum = (left_low.astype(F32) + low.astype(F32)).astype(BF16)
    from_left_top = lax.ppermute(right_sum, "tensor", RIGHT)
    from_right_low = lax.ppermute(left_sum, "tensor", LEFT)
    return from_left_top, from_left_low, from_right_top, from_right_low


def per_device(
    queries,
    rotated_key_rows,
    value_matrix,
    residual,
    lengths,
    move_plan,
    out_weight,
    norm_gain,
    routes,
    bin_slots,
    dropped,
    route_weight,
    gate_weight,
    up_weight,
    down_weight,
):
    x = lax.axis_index("tensor")
    d = lax.axis_index(DP)
    x_ref = jnp.reshape(x, (1,)).astype(jnp.int32)

    weight = lax.all_gather(out_weight, ("y", "core"), axis=0, tiled=False)

    sent = pl.pallas_call(
        attend_kernel,
        out_shape=jax.ShapeDtypeStruct((4, 4, 2, 16, PART + 256), BF16),
        in_specs=[whole(pltpu.SMEM)] * 2 + [whole(pl.ANY)] * 4,
        out_specs=whole(),
        scratch_shapes=[
            pltpu.VMEM((ROWS, PART), BF16),
            pltpu.VMEM((ROWS, HEAD_WIDTH), BF16),
            pltpu.VMEM((ROWS, HEAD_WIDTH), BF16),
            pltpu.VMEM((ROWS, PART), BF16),
            pltpu.SemaphoreType.DMA((4,)),
        ],
        compiler_params=params(VMEM),
        cost_estimate=NO_COST,
        name="attend",
    )(jnp.reshape(d, (1,)).astype(jnp.int32), lengths.T, queries, rotated_key_rows, value_matrix, residual)
    spread = lax.all_to_all(sent.reshape(32, 16, PART + 256), DP, 0, 0, tiled=True)
    spread = spread.reshape(512, PART + 256)

    send0, send1, mix = pl.pallas_call(
        tables_kernel,
        out_shape=[jax.ShapeDtypeStruct((BINS, ROWS), BF16)] * 2
        + [jax.ShapeDtypeStruct((ROWS, 2 * BINS), BF16)],
        in_specs=[whole()] * 7,
        out_specs=[whole()] * 3,
        compiler_params=params(VMEM),
        cost_estimate=NO_COST,
        name="tables",
    )(routes.T, bin_slots.T, dropped.T, routes, bin_slots, dropped, route_weight)
    own_gain = norm_gain.reshape(1, PART)
    far0, far1 = run_columns(x_ref, down_weight, own_gain, ((2, 0), (2, 1)), 1)
    far_w0 = lax.ppermute(lax.ppermute(far0, "tensor", RIGHT), "tensor", RIGHT)
    far_w1 = lax.ppermute(lax.ppermute(far1, "tensor", LEFT), "tensor", LEFT)
    for_right, for_left = run_columns(x_ref, down_weight, own_gain, ((1, 0), (3, 0)), 2, sent)
    (weight,) = after((weight,), far_w0, far_w1, for_right, for_left, send0)

    half = jax.ShapeDtypeStruct((256, 256), BF16)
    *partial, mine = pl.pallas_call(
        project_kernel,
        out_shape=[half] * 6 + [jax.ShapeDtypeStruct((512, 256), F32)],
        in_specs=[whole(pltpu.SMEM)] + [whole()] * 2,
        out_specs=[whole()] * 7,
        compiler_params=params(VMEM),
        cost_estimate=NO_COST,
        name="project",
    )(x_ref, spread, weight)
    sums = ring_scatter(*partial)
    onward = pl.pallas_call(
        route_kernel,
        out_shape=jax.ShapeDtypeStruct((32, 16, 256), BF16),
        in_specs=[whole(pltpu.SMEM)] + [whole()] * 5,
        out_specs=whole(),
        scratch_shapes=[pltpu.VMEM((32, 16, 256), F32)],
        compiler_params=params(VMEM),
        cost_estimate=NO_COST,
        name="route",
    )(move_plan, mine, *sums)
    landed = lax.all_to_all(onward, DP, 0, 0, tiled=True)
    for_right, for_left = after((for_right, for_left), onward)
    left_w = lax.ppermute(for_right, "tensor", RIGHT)
    right_w = lax.ppermute(for_left, "tensor", LEFT)

    stream, bins0 = pl.pallas_call(
        stream_kernel,
        out_shape=[
            jax.ShapeDtypeStruct((ROWS, PART), BF16),
            jax.ShapeDtypeStruct((BINS, PART), BF16),
        ],
        in_specs=[whole()] * 2,
        out_specs=[whole()] * 2,
        compiler_params=params(VMEM),
        cost_estimate=NO_COST,
        name="stream",
    )(landed.reshape(4, 4, 2, 16, 256), send0)
    bins1 = jnp.dot(send1, stream, preferred_element_type=F32).astype(BF16)

    def exchange(rows):
        return lax.all_to_all(rows.reshape(32, CAP, PART), DP, 0, 0, tiled=True).reshape(BINS, PART)

    (held0,) = after((exchange(bins0),), left_w, right_w)

    def whole_gain(rows):
        return jnp.sum(rows[-16:].astype(F32), axis=0, keepdims=True)

    gains = jnp.stack([own_gain, whole_gain(right_w), whole_gain(left_w), whole_gain(far_w0)], axis=0)
    weights = (gate_weight, up_weight)
    right0, left0, top0, low0 = ring_gather(held0)
    partial0 = run_near(x_ref, 0, (held0, right0, left0), gains, *weights)
    (held1,) = after((exchange(bins1),), top0, low0, partial0[1])
    hidden0 = run_far(x_ref, 0, (top0, low0), partial0, gains, *weights)
    right1, left1, top1, low1 = ring_gather(held1, done=(hidden0,))
    partial1 = run_near(x_ref, 1, (held1, right1, left1), gains, *weights)
    (hidden0,) = after((hidden0,), partial1[1])
    units0 = ring_gather(hidden0)
    hidden1 = run_far(x_ref, 1, (top1, low1), partial1, gains, *weights)
    units1 = ring_gather(hidden1)
    back = run_down(x_ref, 0, (hidden0, *units0), down_weight, right_w, left_w, far_w0)
    back = run_down(x_ref, 1, (hidden1, *units1), down_weight, right_w, left_w, far_w1, into=back)
    back = lax.all_to_all(back.reshape(32, 2 * CAP, PART), DP, 0, 0, tiled=True)
    result = jnp.dot(mix, back.reshape(2 * BINS, PART), preferred_element_type=F32)
    return (stream, result.astype(BF16))


def solution(mesh):
    fine = Mesh(mesh.devices.reshape(4, 4, 2, 4), ("y", "z", "core", "tensor"))
    return jax.shard_map(
        per_device,
        mesh=fine,
        in_specs=(
            P(DP, "tensor"),
            P(DP, "tensor"),
            P(DP, "tensor"),
            P(DP, "tensor"),
            P(),
            P(),
            P("tensor", DP),
            P("tensor"),
            P(DP, None),
            P(DP, None),
            P(DP, None),
            P(DP, None),
            P(DP, None, "tensor"),
            P(DP, None, "tensor"),
            P(DP, "tensor", None),
        ),
        out_specs=(P(DP, "tensor"), P(DP, "tensor")),
        check_vma=False,
    )
```

```python
import functools

import jax
import jax.numpy as jnp
from jax import lax
from jax.experimental import pallas as pl
from jax.experimental.pallas import tpu as pltpu
from jax.sharding import Mesh, PartitionSpec as P

D = 4096
HEAD_WIDTH = 128
PACK_ROWS = 64
QUERY_PER_KEY = 8
DP = ("y", "z", "core")
ROWS = 128
CAP = 16
BINS = 32 * CAP
PART = 1024
VMEM = 60
UNITS = 384
F32 = jnp.float32
BF16 = jnp.bfloat16

RIGHT = [(i, (i + 1) % 4) for i in range(4)]
LEFT = [(i, (i - 1) % 4) for i in range(4)]


NO_COST = pl.CostEstimate(flops=0, bytes_accessed=0, transcendentals=0)


def iota(shape, dim):
    return lax.broadcasted_iota(jnp.int32, shape, dim)


def whole(memory_space=pltpu.VMEM):
    return pl.BlockSpec(memory_space=memory_space)


def params(megabytes):
    return pltpu.CompilerParams(vmem_limit_bytes=megabytes << 20)


def after(values, *done):
    count = len(values)
    return pl.pallas_call(
        lambda *refs: None,
        out_shape=[jax.ShapeDtypeStruct(v.shape, v.dtype) for v in values],
        in_specs=[whole(pltpu.HBM)] * (count + len(done)),
        out_specs=[whole(pltpu.HBM)] * count,
        input_output_aliases={i: i for i in range(count)},
        name="after",
    )(*values, *done)


def attend_kernel(
    index, lengths, queries_in, keys_in, values_in, residual_in, out, queries, keys, values, residual, sems
):
    pairs = ((queries_in, queries), (keys_in, keys), (values_in, values), (residual_in, residual))
    copies = [pltpu.make_async_copy(a, b, sems.at[i]) for i, (a, b) in enumerate(pairs)]
    for copy in copies:
        copy.start()
    first = 2 * index[0]
    position = iota((ROWS, ROWS), 0)
    other = iota((ROWS, ROWS), 1)

    def label(at):
        second = at >= PACK_ROWS
        inner = jnp.where(second, at - PACK_ROWS, at)
        found = jnp.where(second, 8, 0)
        ends = [jnp.int32(0), jnp.int32(0)]
        for doc in range(4):
            for s in range(2):
                ends[s] = ends[s] + lengths[doc, first + s]
            found = found + (inner >= jnp.where(second, ends[1], ends[0])).astype(jnp.int32)
        return found

    hidden = jnp.where((label(position) == label(other)) & (position >= other), 0.0, -1e30)
    for copy in copies:
        copy.wait()
    lanes = [slice(h * HEAD_WIDTH, (h + 1) * HEAD_WIDTH) for h in range(QUERY_PER_KEY)]
    stacked = jnp.concatenate([queries[:, part] for part in lanes], axis=0)
    scores = lax.dot_general(
        stacked, keys[...], (((1,), (1,)), ((), ())), preferred_element_type=F32
    ).reshape(QUERY_PER_KEY, ROWS, ROWS)
    masked = jnp.where(hidden[None] < 0.0, -1e30, scores * HEAD_WIDTH**-0.5)
    exps = jnp.exp(masked - jnp.max(masked, axis=2, keepdims=True))
    probs = (exps / jnp.sum(exps, axis=2, keepdims=True)).astype(BF16)
    heads = jnp.dot(
        probs.reshape(QUERY_PER_KEY * ROWS, ROWS), values[...], preferred_element_type=F32
    )
    attended = jnp.concatenate(
        [heads[h * ROWS : (h + 1) * ROWS] for h in range(QUERY_PER_KEY)], axis=1
    )
    rest = residual[...].astype(F32)

    def group(rows, at):
        low = rows[at * 8 : at * 8 + 8]
        high = rows[PACK_ROWS + at * 8 : PACK_ROWS + at * 8 + 8]
        return jnp.concatenate([low, high], axis=0).astype(BF16)

    for y in range(4):
        for core in range(2):
            mine = group(attended, y * 2 + core)
            plain = group(rest, y * 2 + core)
            for z in range(4):
                out[y, z, core, :, :PART] = mine
                out[y, z, core, :, PART:] = plain[:, z * 256 : z * 256 + 256]


def columns_kernel(distances, count, index, weight, gain, *rest):
    outs, sems = rest[-1 - len(distances) : -1], rest[-1]
    copies = []
    for n, (distance, first) in enumerate(distances):
        start = pl.multiple_of(((index[0] + distance) % 4) * PART, PART)
        for i in range(count):
            copies.append(
                pltpu.make_async_copy(
                    weight.at[first + i, :, pl.ds(start, PART)],
                    outs[n].at[pl.ds(i * UNITS, UNITS)],
                    sems.at[n * count + i],
                )
            )
    for copy in copies:
        copy.start()
    left = jnp.broadcast_to(gain[...], (16, PART))
    row = iota((16, PART), 0)
    terms = jnp.zeros((16, PART), F32)
    for k in range(3):
        term = left.astype(BF16).astype(F32)
        terms = jnp.where(row == k, term, terms)
        left = left - term
    for out in outs:
        out[pl.ds(count * UNITS, 16), :] = terms.astype(BF16)
    for copy in copies:
        copy.wait()


def run_columns(x, weight, gain, distances, count, *done):
    rows = count * UNITS + 16
    return pl.pallas_call(
        functools.partial(columns_kernel, distances, count),
        out_shape=[jax.ShapeDtypeStruct((rows, PART), BF16)] * len(distances),
        in_specs=[whole(pltpu.SMEM), whole(pltpu.HBM), whole()] + [whole(pltpu.HBM)] * len(done),
        out_specs=[whole()] * len(distances),
        scratch_shapes=[pltpu.SemaphoreType.DMA((len(distances) * count,))],
        compiler_params=params(VMEM),
        cost_estimate=NO_COST,
        name="columns",
    )(x, weight, gain, *done)


def project_kernel(
    index, rows, weight, done0, done1, far_top, far_low, right_top, right_low, left_top, left_low, mine
):
    def product(distance):
        first = ((index[0] + distance) % 4) * 2
        columns = jnp.concatenate([weight[first], weight[first + 1]], axis=1)
        return jnp.dot(rows[:, :PART], columns, preferred_element_type=F32)

    for distance, upper, lower in ((2, far_top, far_low), (1, right_top, right_low), (3, left_top, left_low)):
        result = product(distance).astype(BF16)
        upper[...] = result[:256]
        lower[...] = result[256:]
    mine[...] = product(0) + rows[:, PART:].astype(F32)


def route_kernel(plan, own, one_top, one_low, two_top, two_low, out, placed):
    top = own[:256] + (one_top[...].astype(F32) + two_top[...].astype(F32))
    low = own[256:] + (one_low[...].astype(F32) + two_low[...].astype(F32))
    for source in range(32):
        at = source * 16
        half = top[at : at + 16] if at < 256 else low[at - 256 : at - 240]
        merged = half.astype(BF16).astype(F32)
        for s in range(2):
            placed[plan[source * 2 + s], s * 8 : s * 8 + 8, :] = merged[s * 8 : s * 8 + 8]
    out[...] = placed[...].astype(BF16)


def stream_kernel(landed, table, stream, bins):
    parts = []
    for z in range(4):
        tiles = [landed[y, z, core].astype(F32) for y in range(4) for core in range(2)]
        parts.append(
            jnp.concatenate([t[s * 8 : s * 8 + 8] for s in range(2) for t in tiles], axis=0)
        )
    rows = jnp.concatenate(parts, axis=1).astype(BF16)
    stream[...] = rows
    bins[...] = jnp.dot(table[...], rows, preferred_element_type=F32).astype(BF16)


def tables_kernel(
    routes_t, slots_t, dropped_t, routes, slots, dropped, weight, send0, send1, mix
):
    across = jnp.where(dropped_t[...] == 0, (routes_t[...] // 2) * CAP + slots_t[...], -1)
    row = iota((BINS, ROWS), 0)
    for local, out in enumerate((send0, send1)):
        mine = jnp.where(routes_t[...] % 2 == local, across, -1)
        total = jnp.zeros((BINS, ROWS), F32)
        for k in range(8):
            total = total + jnp.where(mine[k : k + 1] == row, 1.0, 0.0)
        out[...] = total.astype(BF16)
    down = jnp.where(dropped[...] == 0, routes[...] * CAP + slots[...], -1)
    column = iota((ROWS, 2 * BINS), 1)
    total = jnp.zeros((ROWS, 2 * BINS), F32)
    for k in range(8):
        total = total + jnp.where(down[:, k : k + 1] == column, weight[:, k : k + 1], 0.0)
    mix[...] = total.astype(BF16)


def near_kernel(index, own, right, left, gain, gate_w, up_w, total, squares, rows, sems):
    step = pl.program_id(0)
    copies = [
        pltpu.make_async_copy(source, rows.at[i], sems.at[i])
        for i, source in enumerate((own, right, left))
    ]

    @pl.when(step == 0)
    def _():
        for copy in copies:
            copy.start()
        total[...] = jnp.zeros_like(total)
        squares[...] = jnp.zeros_like(squares)
        copies[0].wait()

    @pl.when(step == 1)
    def _():
        copies[1].wait()

    @pl.when(step == 2)
    def _():
        copies[2].wait()

    wide = rows[step].astype(F32)
    squares[...] += jnp.sum(wide * wide, axis=1, keepdims=True)
    scaled = (wide * gain[...]).astype(BF16)
    both = jnp.concatenate([gate_w[...], up_w[...]], axis=1)
    total[...] += jnp.dot(scaled, both, preferred_element_type=F32)


def far_kernel(index, top, low, total, squares, gain, gate_w, up_w, hidden):
    wide = jnp.concatenate([top[...], low[...]], axis=0).astype(F32)
    mean = (squares[...] + jnp.sum(wide * wide, axis=1, keepdims=True)) * (1.0 / D)
    norm = lax.rsqrt(mean + 1e-6)
    scaled = (wide * gain[...]).astype(BF16)
    both = jnp.concatenate([gate_w[...], up_w[...]], axis=1)
    values = (total[...] + jnp.dot(scaled, both, preferred_element_type=F32)) * norm
    gate = values[:, :UNITS]
    hidden[...] = (gate / (1.0 + jnp.exp(-gate)) * values[:, UNITS:]).astype(BF16)


def flat(shape):
    return pl.BlockSpec(shape, lambda i, at: (0, 0))


def gain_at(slot):
    return pl.BlockSpec((None, 1, PART), lambda i, at: (slot(i), 0, 0))


def weights_at(local, place):
    return [pl.BlockSpec((None, PART, UNITS), lambda i, at: (local, place(i, at), 0))] * 2


def run_near(x, local, blocks, gains, gate_weight, up_weight):
    return pl.pallas_call(
        near_kernel,
        grid_spec=pltpu.PrefetchScalarGridSpec(
            num_scalar_prefetch=1,
            grid=(3,),
            in_specs=[whole(pltpu.HBM)] * 3
            + [gain_at(lambda i: i)]
            + weights_at(local, lambda i, at: (at[0] + (i ^ (i >> 1))) % 4),
            out_specs=[flat((BINS, 2 * UNITS)), flat((BINS, 1))],
            scratch_shapes=[pltpu.VMEM((3, BINS, PART), BF16), pltpu.SemaphoreType.DMA((3,))],
        ),
        out_shape=[
            jax.ShapeDtypeStruct((BINS, 2 * UNITS), F32),
            jax.ShapeDtypeStruct((BINS, 1), F32),
        ],
        compiler_params=params(VMEM),
        cost_estimate=NO_COST,
        name="near",
    )(x, *blocks, gains, gate_weight, up_weight)


def run_far(x, local, blocks, near, gains, gate_weight, up_weight):
    return pl.pallas_call(
        far_kernel,
        grid_spec=pltpu.PrefetchScalarGridSpec(
            num_scalar_prefetch=1,
            grid=(1,),
            in_specs=[flat(v.shape) for v in (*blocks, *near)]
            + [gain_at(lambda i: 3)]
            + weights_at(local, lambda i, at: (at[0] + 2) % 4),
            out_specs=flat((BINS, UNITS)),
        ),
        out_shape=jax.ShapeDtypeStruct((BINS, UNITS), BF16),
        compiler_params=params(VMEM),
        cost_estimate=NO_COST,
        name="far",
    )(x, *blocks, *near, gains, gate_weight, up_weight)


def down_kernel(
    local, index, own, right, left, top, low, own_w, right_w, left_w, far_w, *rest
):
    out, units, weights, product, sems = rest[-5:]
    half = BINS // 2
    column = pl.multiple_of(index[0] * PART, PART)
    rows = pl.ds(local * UNITS, UNITS)
    pairs = (
        (own, units.at[0]),
        (own_w.at[local, :, pl.ds(column, PART)], weights.at[0]),
        (right, units.at[1]),
        (right_w.at[rows], weights.at[1]),
        (left, units.at[2]),
        (left_w.at[rows], weights.at[2]),
        (top, units.at[3, pl.ds(0, half)]),
        (low, units.at[3, pl.ds(half, half)]),
        (far_w.at[pl.ds(0, UNITS)], weights.at[3]),
    )
    copies = [pltpu.make_async_copy(a, b, sems.at[i]) for i, (a, b) in enumerate(pairs)]
    for copy in copies:
        copy.start()
    total = 0.0
    for block in range(4):
        for copy in copies[2 * block : 2 * block + (3 if block == 3 else 2)]:
            copy.wait()
        total = total + jnp.dot(units[block], weights[block], preferred_element_type=F32)
    product[...] = total.astype(BF16).reshape(32, CAP, PART)
    result = pltpu.make_async_copy(product, out.at[:, local], sems.at[9])
    result.start()
    result.wait()


def run_down(x, local, blocks, down_weight, right_w, left_w, far_w, *more, into=None):
    given = (*blocks, down_weight, right_w, left_w, far_w, *more) + (() if into is None else (into,))
    return pl.pallas_call(
        functools.partial(down_kernel, local),
        out_shape=jax.ShapeDtypeStruct((32, 2, CAP, PART), BF16),
        in_specs=[whole(pltpu.SMEM)] + [whole(pl.ANY)] * len(given),
        out_specs=whole(pltpu.HBM),
        input_output_aliases={} if into is None else {len(given): 0},
        scratch_shapes=[
            pltpu.VMEM((4, BINS, UNITS), BF16),
            pltpu.VMEM((4, UNITS, PART), BF16),
            pltpu.VMEM((32, CAP, PART), BF16),
            pltpu.SemaphoreType.DMA((10,)),
        ],
        compiler_params=params(VMEM),
        cost_estimate=NO_COST,
        name="down",
    )(x, *given)


def ring_gather(block, axis="tensor", done=()):
    half = block.shape[0] // 2
    left = lax.ppermute(block, axis, RIGHT)
    right = lax.ppermute(block, axis, LEFT)
    upper, lower = left[:half], right[half:]
    if done:
        upper, lower = after((upper, lower), *done)
    return right, left, lax.ppermute(upper, axis, RIGHT), lax.ppermute(lower, axis, LEFT)


def ring_scatter(far_top, far_low, right_top, right_low, left_top, left_low):
    top = lax.ppermute(far_top, "tensor", RIGHT)
    low = lax.ppermute(far_low, "tensor", LEFT)
    from_left_low = lax.ppermute(right_low, "tensor", RIGHT)
    from_right_top = lax.ppermute(left_top, "tensor", LEFT)
    right_sum = (right_top.astype(F32) + top.astype(F32)).astype(BF16)
    left_sum = (left_low.astype(F32) + low.astype(F32)).astype(BF16)
    from_left_top = lax.ppermute(right_sum, "tensor", RIGHT)
    from_right_low = lax.ppermute(left_sum, "tensor", LEFT)
    return from_left_top, from_left_low, from_right_top, from_right_low


def per_device(
    queries,
    rotated_key_rows,
    value_matrix,
    residual,
    lengths,
    move_plan,
    out_weight,
    norm_gain,
    routes,
    bin_slots,
    dropped,
    route_weight,
    gate_weight,
    up_weight,
    down_weight,
):
    x = lax.axis_index("tensor")
    d = lax.axis_index(DP)
    x_ref = jnp.reshape(x, (1,)).astype(jnp.int32)

    weight = lax.all_gather(out_weight, ("y", "core"), axis=0, tiled=False)

    sent = pl.pallas_call(
        attend_kernel,
        out_shape=jax.ShapeDtypeStruct((4, 4, 2, 16, PART + 256), BF16),
        in_specs=[whole(pltpu.SMEM)] * 2 + [whole(pl.ANY)] * 4,
        out_specs=whole(),
        scratch_shapes=[
            pltpu.VMEM((ROWS, PART), BF16),
            pltpu.VMEM((ROWS, HEAD_WIDTH), BF16),
            pltpu.VMEM((ROWS, HEAD_WIDTH), BF16),
            pltpu.VMEM((ROWS, PART), BF16),
            pltpu.SemaphoreType.DMA((4,)),
        ],
        compiler_params=params(VMEM),
        cost_estimate=NO_COST,
        name="attend",
    )(jnp.reshape(d, (1,)).astype(jnp.int32), lengths.T, queries, rotated_key_rows, value_matrix, residual)
    spread = lax.all_to_all(sent.reshape(32, 16, PART + 256), DP, 0, 0, tiled=True)
    spread = spread.reshape(512, PART + 256)

    send0, send1, mix = pl.pallas_call(
        tables_kernel,
        out_shape=[jax.ShapeDtypeStruct((BINS, ROWS), BF16)] * 2
        + [jax.ShapeDtypeStruct((ROWS, 2 * BINS), BF16)],
        in_specs=[whole()] * 7,
        out_specs=[whole()] * 3,
        compiler_params=params(VMEM),
        cost_estimate=NO_COST,
        name="tables",
    )(routes.T, bin_slots.T, dropped.T, routes, bin_slots, dropped, route_weight)
    own_gain = norm_gain.reshape(1, PART)
    far0, far1 = run_columns(x_ref, down_weight, own_gain, ((2, 0), (2, 1)), 1)
    far_w0 = lax.ppermute(lax.ppermute(far0, "tensor", RIGHT), "tensor", RIGHT)
    far_w1 = lax.ppermute(lax.ppermute(far1, "tensor", LEFT), "tensor", LEFT)
    for_right, for_left = run_columns(x_ref, down_weight, own_gain, ((1, 0), (3, 0)), 2, sent)
    (weight,) = after((weight,), for_right, for_left, send0)

    half = jax.ShapeDtypeStruct((256, 256), BF16)
    *partial, mine = pl.pallas_call(
        project_kernel,
        out_shape=[half] * 6 + [jax.ShapeDtypeStruct((512, 256), F32)],
        in_specs=[whole(pltpu.SMEM)] + [whole()] * 2 + [whole(pltpu.HBM)] * 2,
        out_specs=[whole()] * 7,
        compiler_params=params(VMEM),
        cost_estimate=NO_COST,
        name="project",
    )(x_ref, spread, weight, far_w0, far_w1)
    sums = ring_scatter(*partial)
    onward = pl.pallas_call(
        route_kernel,
        out_shape=jax.ShapeDtypeStruct((32, 16, 256), BF16),
        in_specs=[whole(pltpu.SMEM)] + [whole()] * 5,
        out_specs=whole(),
        scratch_shapes=[pltpu.VMEM((32, 16, 256), F32)],
        compiler_params=params(VMEM),
        cost_estimate=NO_COST,
        name="route",
    )(move_plan, mine, *sums)
    landed = lax.all_to_all(onward, DP, 0, 0, tiled=True)
    for_right, for_left = after((for_right, for_left), onward)
    left_w = lax.ppermute(for_right, "tensor", RIGHT)
    right_w = lax.ppermute(for_left, "tensor", LEFT)

    stream, bins0 = pl.pallas_call(
        stream_kernel,
        out_shape=[
            jax.ShapeDtypeStruct((ROWS, PART), BF16),
            jax.ShapeDtypeStruct((BINS, PART), BF16),
        ],
        in_specs=[whole()] * 2,
        out_specs=[whole()] * 2,
        compiler_params=params(VMEM),
        cost_estimate=NO_COST,
        name="stream",
    )(landed.reshape(4, 4, 2, 16, 256), send0)
    bins1 = jnp.dot(send1, stream, preferred_element_type=F32).astype(BF16)

    def exchange(rows):
        return lax.all_to_all(rows.reshape(32, CAP, PART), DP, 0, 0, tiled=True).reshape(BINS, PART)

    (held0,) = after((exchange(bins0),), left_w, right_w)

    def whole_gain(rows):
        return jnp.sum(rows[-16:].astype(F32), axis=0, keepdims=True)

    gains = jnp.stack([own_gain, whole_gain(right_w), whole_gain(left_w), whole_gain(far_w0)], axis=0)
    weights = (gate_weight, up_weight)
    right0, left0, top0, low0 = ring_gather(held0)
    partial0 = run_near(x_ref, 0, (held0, right0, left0), gains, *weights)
    (held1,) = after((exchange(bins1),), top0, low0, partial0[1])
    hidden0 = run_far(x_ref, 0, (top0, low0), partial0, gains, *weights)
    right1, left1, top1, low1 = ring_gather(held1, done=(hidden0,))
    partial1 = run_near(x_ref, 1, (held1, right1, left1), gains, *weights)
    (hidden0,) = after((hidden0,), partial1[1])
    units0 = ring_gather(hidden0)
    hidden1 = run_far(x_ref, 1, (top1, low1), partial1, gains, *weights)
    units1 = ring_gather(hidden1)
    back = run_down(x_ref, 0, (hidden0, *units0), down_weight, right_w, left_w, far_w0)
    back = run_down(x_ref, 1, (hidden1, *units1), down_weight, right_w, left_w, far_w1, into=back)
    back = lax.all_to_all(back.reshape(32, 2 * CAP, PART), DP, 0, 0, tiled=True)
    result = jnp.dot(mix, back.reshape(2 * BINS, PART), preferred_element_type=F32)
    return (stream, result.astype(BF16))


def solution(mesh):
    fine = Mesh(mesh.devices.reshape(4, 4, 2, 4), ("y", "z", "core", "tensor"))
    return jax.shard_map(
        per_device,
        mesh=fine,
        in_specs=(
            P(DP, "tensor"),
            P(DP, "tensor"),
            P(DP, "tensor"),
            P(DP, "tensor"),
            P(),
            P(),
            P("tensor", DP),
            P("tensor"),
            P(DP, None),
            P(DP, None),
            P(DP, None),
            P(DP, None),
            P(DP, None, "tensor"),
            P(DP, None, "tensor"),
            P(DP, "tensor", None),
        ),
        out_specs=(P(DP, "tensor"), P(DP, "tensor")),
        check_vma=False,
    )
```

```python
import functools

import jax
import jax.numpy as jnp
from jax import lax
from jax.experimental import pallas as pl
from jax.experimental.pallas import tpu as pltpu
from jax.sharding import Mesh, PartitionSpec as P

D = 4096
HEAD_WIDTH = 128
PACK_ROWS = 64
QUERY_PER_KEY = 8
DP = ("y", "z", "core")
ROWS = 128
CAP = 16
BINS = 32 * CAP
PART = 1024
VMEM = 60
UNITS = 384
F32 = jnp.float32
BF16 = jnp.bfloat16

RIGHT = [(i, (i + 1) % 4) for i in range(4)]
LEFT = [(i, (i - 1) % 4) for i in range(4)]


NO_COST = pl.CostEstimate(flops=0, bytes_accessed=0, transcendentals=0)


def iota(shape, dim):
    return lax.broadcasted_iota(jnp.int32, shape, dim)


def whole(memory_space=pltpu.VMEM):
    return pl.BlockSpec(memory_space=memory_space)


def params(megabytes):
    return pltpu.CompilerParams(vmem_limit_bytes=megabytes << 20)


def after(values, *done):
    count = len(values)
    return pl.pallas_call(
        lambda *refs: None,
        out_shape=[jax.ShapeDtypeStruct(v.shape, v.dtype) for v in values],
        in_specs=[whole(pltpu.HBM)] * (count + len(done)),
        out_specs=[whole(pltpu.HBM)] * count,
        input_output_aliases={i: i for i in range(count)},
        name="after",
    )(*values, *done)


def attend_kernel(
    index, lengths, queries_in, keys_in, values_in, residual_in, out, queries, keys, values, residual, sems
):
    pairs = ((queries_in, queries), (keys_in, keys), (values_in, values), (residual_in, residual))
    copies = [pltpu.make_async_copy(a, b, sems.at[i]) for i, (a, b) in enumerate(pairs)]
    for copy in copies:
        copy.start()
    first = 2 * index[0]
    position = iota((ROWS, ROWS), 0)
    other = iota((ROWS, ROWS), 1)

    def label(at):
        second = at >= PACK_ROWS
        inner = jnp.where(second, at - PACK_ROWS, at)
        found = jnp.where(second, 8, 0)
        ends = [jnp.int32(0), jnp.int32(0)]
        for doc in range(4):
            for s in range(2):
                ends[s] = ends[s] + lengths[doc, first + s]
            found = found + (inner >= jnp.where(second, ends[1], ends[0])).astype(jnp.int32)
        return found

    hidden = jnp.where((label(position) == label(other)) & (position >= other), 0.0, -1e30)
    for copy in copies:
        copy.wait()
    lanes = [slice(h * HEAD_WIDTH, (h + 1) * HEAD_WIDTH) for h in range(QUERY_PER_KEY)]
    stacked = jnp.concatenate([queries[:, part] for part in lanes], axis=0)
    scores = lax.dot_general(
        stacked, keys[...], (((1,), (1,)), ((), ())), preferred_element_type=F32
    ).reshape(QUERY_PER_KEY, ROWS, ROWS)
    masked = jnp.where(hidden[None] < 0.0, -1e30, scores * HEAD_WIDTH**-0.5)
    exps = jnp.exp(masked - jnp.max(masked, axis=2, keepdims=True))
    probs = (exps / jnp.sum(exps, axis=2, keepdims=True)).astype(BF16)
    heads = jnp.dot(
        probs.reshape(QUERY_PER_KEY * ROWS, ROWS), values[...], preferred_element_type=F32
    )
    attended = jnp.concatenate(
        [heads[h * ROWS : (h + 1) * ROWS] for h in range(QUERY_PER_KEY)], axis=1
    )
    rest = residual[...].astype(F32)

    def group(rows, at):
        low = rows[at * 8 : at * 8 + 8]
        high = rows[PACK_ROWS + at * 8 : PACK_ROWS + at * 8 + 8]
        return jnp.concatenate([low, high], axis=0).astype(BF16)

    for y in range(4):
        for core in range(2):
            mine = group(attended, y * 2 + core)
            plain = group(rest, y * 2 + core)
            for z in range(4):
                out[y, z, core, :, :PART] = mine
                out[y, z, core, :, PART:] = plain[:, z * 256 : z * 256 + 256]


def columns_kernel(distances, count, index, weight, gain, *rest):
    outs, sems = rest[-1 - len(distances) : -1], rest[-1]
    copies = []
    for n, (distance, first) in enumerate(distances):
        start = pl.multiple_of(((index[0] + distance) % 4) * PART, PART)
        for i in range(count):
            copies.append(
                pltpu.make_async_copy(
                    weight.at[first + i, :, pl.ds(start, PART)],
                    outs[n].at[pl.ds(i * UNITS, UNITS)],
                    sems.at[n * count + i],
                )
            )
    for copy in copies:
        copy.start()
    left = jnp.broadcast_to(gain[...], (16, PART))
    row = iota((16, PART), 0)
    terms = jnp.zeros((16, PART), F32)
    for k in range(3):
        term = left.astype(BF16).astype(F32)
        terms = jnp.where(row == k, term, terms)
        left = left - term
    for out in outs:
        out[pl.ds(count * UNITS, 16), :] = terms.astype(BF16)
    for copy in copies:
        copy.wait()


def run_columns(x, weight, gain, distances, count, *done):
    rows = count * UNITS + 16
    return pl.pallas_call(
        functools.partial(columns_kernel, distances, count),
        out_shape=[jax.ShapeDtypeStruct((rows, PART), BF16)] * len(distances),
        in_specs=[whole(pltpu.SMEM), whole(pltpu.HBM), whole()] + [whole(pltpu.HBM)] * len(done),
        out_specs=[whole()] * len(distances),
        scratch_shapes=[pltpu.SemaphoreType.DMA((len(distances) * count,))],
        compiler_params=params(VMEM),
        cost_estimate=NO_COST,
        name="columns",
    )(x, weight, gain, *done)


def project_kernel(
    index, rows, weight, done0, done1, far_top, far_low, right_top, right_low, left_top, left_low, mine
):
    def product(distance):
        first = ((index[0] + distance) % 4) * 2
        columns = jnp.concatenate([weight[first], weight[first + 1]], axis=1)
        return jnp.dot(rows[:, :PART], columns, preferred_element_type=F32)

    for distance, upper, lower in ((2, far_top, far_low), (1, right_top, right_low), (3, left_top, left_low)):
        result = product(distance).astype(BF16)
        upper[...] = result[:256]
        lower[...] = result[256:]
    mine[...] = product(0) + rows[:, PART:].astype(F32)


def route_kernel(plan, own, one_top, one_low, two_top, two_low, out, placed):
    top = own[:256] + (one_top[...].astype(F32) + two_top[...].astype(F32))
    low = own[256:] + (one_low[...].astype(F32) + two_low[...].astype(F32))
    for source in range(32):
        at = source * 16
        half = top[at : at + 16] if at < 256 else low[at - 256 : at - 240]
        merged = half.astype(BF16).astype(F32)
        for s in range(2):
            placed[plan[source * 2 + s], s * 8 : s * 8 + 8, :] = merged[s * 8 : s * 8 + 8]
    out[...] = placed[...].astype(BF16)


def stream_kernel(landed, table, stream, bins):
    parts = []
    for z in range(4):
        tiles = [landed[y, z, core].astype(F32) for y in range(4) for core in range(2)]
        parts.append(
            jnp.concatenate([t[s * 8 : s * 8 + 8] for s in range(2) for t in tiles], axis=0)
        )
    rows = jnp.concatenate(parts, axis=1).astype(BF16)
    stream[...] = rows
    bins[...] = jnp.dot(table[...], rows, preferred_element_type=F32).astype(BF16)


def tables_kernel(
    routes_t, slots_t, dropped_t, routes, slots, dropped, weight, send0, send1, mix
):
    across = jnp.where(dropped_t[...] == 0, (routes_t[...] // 2) * CAP + slots_t[...], -1)
    row = iota((BINS, ROWS), 0)
    for local, out in enumerate((send0, send1)):
        mine = jnp.where(routes_t[...] % 2 == local, across, -1)
        total = jnp.zeros((BINS, ROWS), F32)
        for k in range(8):
            total = total + jnp.where(mine[k : k + 1] == row, 1.0, 0.0)
        out[...] = total.astype(BF16)
    down = jnp.where(dropped[...] == 0, routes[...] * CAP + slots[...], -1)
    column = iota((ROWS, 2 * BINS), 1)
    total = jnp.zeros((ROWS, 2 * BINS), F32)
    for k in range(8):
        total = total + jnp.where(down[:, k : k + 1] == column, weight[:, k : k + 1], 0.0)
    mix[...] = total.astype(BF16)


def near_kernel(index, own, right, left, gain, gate_w, up_w, total, squares, rows, sems):
    step = pl.program_id(0)
    copies = [
        pltpu.make_async_copy(source, rows.at[i], sems.at[i])
        for i, source in enumerate((own, right, left))
    ]

    @pl.when(step == 0)
    def _():
        for copy in copies:
            copy.start()
        total[...] = jnp.zeros_like(total)
        squares[...] = jnp.zeros_like(squares)
        copies[0].wait()

    @pl.when(step == 1)
    def _():
        copies[1].wait()

    @pl.when(step == 2)
    def _():
        copies[2].wait()

    wide = rows[step].astype(F32)
    squares[...] += jnp.sum(wide * wide, axis=1, keepdims=True)
    scaled = (wide * gain[...]).astype(BF16)
    both = jnp.concatenate([gate_w[...], up_w[...]], axis=1)
    total[...] += jnp.dot(scaled, both, preferred_element_type=F32)


def far_kernel(index, top, low, total, squares, gain, gate_w, up_w, hidden):
    wide = jnp.concatenate([top[...], low[...]], axis=0).astype(F32)
    mean = (squares[...] + jnp.sum(wide * wide, axis=1, keepdims=True)) * (1.0 / D)
    norm = lax.rsqrt(mean + 1e-6)
    scaled = (wide * gain[...]).astype(BF16)
    both = jnp.concatenate([gate_w[...], up_w[...]], axis=1)
    values = (total[...] + jnp.dot(scaled, both, preferred_element_type=F32)) * norm
    gate = values[:, :UNITS]
    hidden[...] = (gate / (1.0 + jnp.exp(-gate)) * values[:, UNITS:]).astype(BF16)


def flat(shape):
    return pl.BlockSpec(shape, lambda i, at: (0, 0))


def gain_at(slot):
    return pl.BlockSpec((None, 1, PART), lambda i, at: (slot(i), 0, 0))


def weights_at(local, place):
    return [pl.BlockSpec((None, PART, UNITS), lambda i, at: (local, place(i, at), 0))] * 2


def run_near(x, local, blocks, gains, gate_weight, up_weight):
    return pl.pallas_call(
        near_kernel,
        grid_spec=pltpu.PrefetchScalarGridSpec(
            num_scalar_prefetch=1,
            grid=(3,),
            in_specs=[whole(pltpu.HBM)] * 3
            + [gain_at(lambda i: i)]
            + weights_at(local, lambda i, at: (at[0] + (i ^ (i >> 1))) % 4),
            out_specs=[flat((BINS, 2 * UNITS)), flat((BINS, 1))],
            scratch_shapes=[pltpu.VMEM((3, BINS, PART), BF16), pltpu.SemaphoreType.DMA((3,))],
        ),
        out_shape=[
            jax.ShapeDtypeStruct((BINS, 2 * UNITS), F32),
            jax.ShapeDtypeStruct((BINS, 1), F32),
        ],
        compiler_params=params(VMEM),
        cost_estimate=NO_COST,
        name="near",
    )(x, *blocks, gains, gate_weight, up_weight)


def run_far(x, local, blocks, near, gains, gate_weight, up_weight):
    return pl.pallas_call(
        far_kernel,
        grid_spec=pltpu.PrefetchScalarGridSpec(
            num_scalar_prefetch=1,
            grid=(1,),
            in_specs=[flat(v.shape) for v in (*blocks, *near)]
            + [gain_at(lambda i: 3)]
            + weights_at(local, lambda i, at: (at[0] + 2) % 4),
            out_specs=flat((BINS, UNITS)),
        ),
        out_shape=jax.ShapeDtypeStruct((BINS, UNITS), BF16),
        compiler_params=params(VMEM),
        cost_estimate=NO_COST,
        name="far",
    )(x, *blocks, *near, gains, gate_weight, up_weight)


def down_kernel(
    local, index, own, right, left, top, low, own_w, right_w, left_w, far_w, *rest
):
    out, units, weights, product, sems = rest[-5:]
    half = BINS // 2
    column = pl.multiple_of(index[0] * PART, PART)
    rows = pl.ds(local * UNITS, UNITS)
    pairs = (
        (own, units.at[0]),
        (own_w.at[local, :, pl.ds(column, PART)], weights.at[0]),
        (right, units.at[1]),
        (right_w.at[rows], weights.at[1]),
        (left, units.at[2]),
        (left_w.at[rows], weights.at[2]),
        (top, units.at[3, pl.ds(0, half)]),
        (low, units.at[3, pl.ds(half, half)]),
        (far_w.at[pl.ds(0, UNITS)], weights.at[3]),
    )
    copies = [pltpu.make_async_copy(a, b, sems.at[i]) for i, (a, b) in enumerate(pairs)]
    for copy in copies:
        copy.start()
    total = 0.0
    for block in range(4):
        for copy in copies[2 * block : 2 * block + (3 if block == 3 else 2)]:
            copy.wait()
        total = total + jnp.dot(units[block], weights[block], preferred_element_type=F32)
    product[...] = total.astype(BF16).reshape(32, CAP, PART)
    result = pltpu.make_async_copy(product, out.at[:, local], sems.at[9])
    result.start()
    result.wait()


def run_down(x, local, blocks, down_weight, right_w, left_w, far_w, *more, into=None):
    given = (*blocks, down_weight, right_w, left_w, far_w, *more) + (() if into is None else (into,))
    return pl.pallas_call(
        functools.partial(down_kernel, local),
        out_shape=jax.ShapeDtypeStruct((32, 2, CAP, PART), BF16),
        in_specs=[whole(pltpu.SMEM)] + [whole(pl.ANY)] * len(given),
        out_specs=whole(pltpu.HBM),
        input_output_aliases={} if into is None else {len(given): 0},
        scratch_shapes=[
            pltpu.VMEM((4, BINS, UNITS), BF16),
            pltpu.VMEM((4, UNITS, PART), BF16),
            pltpu.VMEM((32, CAP, PART), BF16),
            pltpu.SemaphoreType.DMA((10,)),
        ],
        compiler_params=params(VMEM),
        cost_estimate=NO_COST,
        name="down",
    )(x, *given)


def ring_gather(block, axis="tensor", done=()):
    half = block.shape[0] // 2
    left = lax.ppermute(block, axis, RIGHT)
    right = lax.ppermute(block, axis, LEFT)
    upper, lower = left[:half], right[half:]
    if done:
        upper, lower = after((upper, lower), *done)
    return right, left, lax.ppermute(upper, axis, RIGHT), lax.ppermute(lower, axis, LEFT)


def ring_scatter(far_top, far_low, right_top, right_low, left_top, left_low):
    top = lax.ppermute(far_top, "tensor", RIGHT)
    low = lax.ppermute(far_low, "tensor", LEFT)
    from_left_low = lax.ppermute(right_low, "tensor", RIGHT)
    from_right_top = lax.ppermute(left_top, "tensor", LEFT)
    right_sum = (right_top.astype(F32) + top.astype(F32)).astype(BF16)
    left_sum = (left_low.astype(F32) + low.astype(F32)).astype(BF16)
    from_left_top = lax.ppermute(right_sum, "tensor", RIGHT)
    from_right_low = lax.ppermute(left_sum, "tensor", LEFT)
    return from_left_top, from_left_low, from_right_top, from_right_low


def per_device(
    queries,
    rotated_key_rows,
    value_matrix,
    residual,
    lengths,
    move_plan,
    out_weight,
    norm_gain,
    routes,
    bin_slots,
    dropped,
    route_weight,
    gate_weight,
    up_weight,
    down_weight,
):
    x = lax.axis_index("tensor")
    d = lax.axis_index(DP)
    x_ref = jnp.reshape(x, (1,)).astype(jnp.int32)

    weight = lax.all_gather(out_weight, ("y", "core"), axis=0, tiled=False)

    sent = pl.pallas_call(
        attend_kernel,
        out_shape=jax.ShapeDtypeStruct((4, 4, 2, 16, PART + 256), BF16),
        in_specs=[whole(pltpu.SMEM)] * 2 + [whole(pl.ANY)] * 4,
        out_specs=whole(),
        scratch_shapes=[
            pltpu.VMEM((ROWS, PART), BF16),
            pltpu.VMEM((ROWS, HEAD_WIDTH), BF16),
            pltpu.VMEM((ROWS, HEAD_WIDTH), BF16),
            pltpu.VMEM((ROWS, PART), BF16),
            pltpu.SemaphoreType.DMA((4,)),
        ],
        compiler_params=params(VMEM),
        cost_estimate=NO_COST,
        name="attend",
    )(jnp.reshape(d, (1,)).astype(jnp.int32), lengths.T, queries, rotated_key_rows, value_matrix, residual)
    spread = lax.all_to_all(sent.reshape(32, 16, PART + 256), DP, 0, 0, tiled=True)
    spread = spread.reshape(512, PART + 256)

    send0, send1, mix = pl.pallas_call(
        tables_kernel,
        out_shape=[jax.ShapeDtypeStruct((BINS, ROWS), BF16)] * 2
        + [jax.ShapeDtypeStruct((ROWS, 2 * BINS), BF16)],
        in_specs=[whole()] * 7,
        out_specs=[whole()] * 3,
        compiler_params=params(VMEM),
        cost_estimate=NO_COST,
        name="tables",
    )(routes.T, bin_slots.T, dropped.T, routes, bin_slots, dropped, route_weight)
    own_gain = norm_gain.reshape(1, PART)
    far0, far1 = run_columns(x_ref, down_weight, own_gain, ((2, 0), (2, 1)), 1)
    far_w0 = lax.ppermute(lax.ppermute(far0, "tensor", RIGHT), "tensor", RIGHT)
    far_w1 = lax.ppermute(lax.ppermute(far1, "tensor", LEFT), "tensor", LEFT)
    for_right, for_left = run_columns(x_ref, down_weight, own_gain, ((1, 0), (3, 0)), 2, sent)
    (weight,) = after((weight,), for_right, for_left, send0)

    half = jax.ShapeDtypeStruct((256, 256), BF16)
    *partial, mine = pl.pallas_call(
        project_kernel,
        out_shape=[half] * 6 + [jax.ShapeDtypeStruct((512, 256), F32)],
        in_specs=[whole(pltpu.SMEM)] + [whole()] * 2 + [whole(pltpu.HBM)] * 2,
        out_specs=[whole()] * 7,
        compiler_params=params(VMEM),
        cost_estimate=NO_COST,
        name="project",
    )(x_ref, spread, weight, far_w0, far_w1)
    sums = ring_scatter(*partial)
    onward = pl.pallas_call(
        route_kernel,
        out_shape=jax.ShapeDtypeStruct((32, 16, 256), BF16),
        in_specs=[whole(pltpu.SMEM)] + [whole()] * 5,
        out_specs=whole(),
        scratch_shapes=[pltpu.VMEM((32, 16, 256), F32)],
        compiler_params=params(VMEM),
        cost_estimate=NO_COST,
        name="route",
    )(move_plan, mine, *sums)
    landed = lax.all_to_all(onward, DP, 0, 0, tiled=True)
    for_right, for_left = after((for_right, for_left), onward)
    left_w = lax.ppermute(for_right, "tensor", RIGHT)
    right_w = lax.ppermute(for_left, "tensor", LEFT)

    stream, bins0 = pl.pallas_call(
        stream_kernel,
        out_shape=[
            jax.ShapeDtypeStruct((ROWS, PART), BF16),
            jax.ShapeDtypeStruct((BINS, PART), BF16),
        ],
        in_specs=[whole()] * 2,
        out_specs=[whole()] * 2,
        compiler_params=params(VMEM),
        cost_estimate=NO_COST,
        name="stream",
    )(landed.reshape(4, 4, 2, 16, 256), send0)
    bins1 = jnp.dot(send1, stream, preferred_element_type=F32).astype(BF16)

    def exchange(rows):
        return lax.all_to_all(rows.reshape(32, CAP, PART), DP, 0, 0, tiled=True).reshape(BINS, PART)

    (held0,) = after((exchange(bins0),), left_w, right_w)

    def whole_gain(rows):
        return jnp.sum(rows[-16:].astype(F32), axis=0, keepdims=True)

    gains = jnp.stack([own_gain, whole_gain(right_w), whole_gain(left_w), whole_gain(far_w0)], axis=0)
    weights = (gate_weight, up_weight)
    right0, left0, top0, low0 = ring_gather(held0)
    partial0 = run_near(x_ref, 0, (held0, right0, left0), gains, *weights)
    (held1,) = after((exchange(bins1),), partial0[1])
    hidden0 = run_far(x_ref, 0, (top0, low0), partial0, gains, *weights)
    right1, left1, top1, low1 = ring_gather(held1, done=(hidden0,))
    partial1 = run_near(x_ref, 1, (held1, right1, left1), gains, *weights)
    (hidden0,) = after((hidden0,), partial1[1])
    units0 = ring_gather(hidden0)
    hidden1 = run_far(x_ref, 1, (top1, low1), partial1, gains, *weights)
    units1 = ring_gather(hidden1)
    back = run_down(x_ref, 0, (hidden0, *units0), down_weight, right_w, left_w, far_w0)
    back = run_down(x_ref, 1, (hidden1, *units1), down_weight, right_w, left_w, far_w1, into=back)
    back = lax.all_to_all(back.reshape(32, 2 * CAP, PART), DP, 0, 0, tiled=True)
    result = jnp.dot(mix, back.reshape(2 * BINS, PART), preferred_element_type=F32)
    return (stream, result.astype(BF16))


def solution(mesh):
    fine = Mesh(mesh.devices.reshape(4, 4, 2, 4), ("y", "z", "core", "tensor"))
    return jax.shard_map(
        per_device,
        mesh=fine,
        in_specs=(
            P(DP, "tensor"),
            P(DP, "tensor"),
            P(DP, "tensor"),
            P(DP, "tensor"),
            P(),
            P(),
            P("tensor", DP),
            P("tensor"),
            P(DP, None),
            P(DP, None),
            P(DP, None),
            P(DP, None),
            P(DP, None, "tensor"),
            P(DP, None, "tensor"),
            P(DP, "tensor", None),
        ),
        out_specs=(P(DP, "tensor"), P(DP, "tensor")),
        check_vma=False,
    )
```
